128 devices in a mesh: seq: 16 (over z, y_lo, core), head: 8 (over x, y_hi).
Axes of the slice: x: 4, y: 4 (y_hi: 2, y_lo: 2; y = y_hi * 2 + y_lo), z: 4, core: 2. Of those that a mesh axis runs over, the one named last changes fastest.
Arguments:
- context_hidden: bfloat16 [32, 1024, 8192], P(None, ('seq', 'head')), may hold values from -25 to 25
- norm_gain: float32 [8192], replicated, may hold values from 0.25 to 1.75
- kv_weight: bfloat16 [2, 8192, 1024], P(None, 'seq', 'head'), may hold values from -0.0625 to 0.0625
- queries: bfloat16 [4, 32, 8192], P(None, None, 'head'), may hold values from -12 to 12
- new_kv: bfloat16 [2, 4, 32, 1024], P(None, None, None, 'head'), may hold values from -12 to 12
- lengths: int32 [32], replicated, may hold values from 1 to 1024, 16384 in all
- slab_start: int32 [32], replicated, may hold values from 0 to 130043
Outputs:
- k_cache: bfloat16 [32, 1024, 1024], P(None, 'seq', 'head')
- v_cache: bfloat16 [32, 1024, 1024], P(None, 'seq', 'head')
- attention: bfloat16 [4, 32, 8192], P(None, 'seq', 'head')
The draws below stay inside these ranges and needn't reach their ends.
Inputs may be any that keep to these rules, and one draw needn't show every extreme that they name: `lengths`: they sum to 16384, and some session reaches 1024.
All inputs are finite; a program needn't handle non-finite values.
Results may differ from the reference program's by a relative error of at most 0.013.
Values may be sent and summed in bfloat16 or wider, within the bound.
No kernel may reach another device: no remote copies, remote signals or barrier semaphores. Data moves between devices by JAX's collectives and lax.ppermute only.
A program may use at most 128 MiB of HBM per device.

```python
import math
import jax
import jax.numpy as jnp
import numpy as np
from jax import lax

D = 8192
HQ = 64
KVH = 8
HD = 128
B = 32
STEPS = 4
CAP = 1024


def strong_rows(key):
    choose_level = jax.random.randint(jax.random.fold_in(key, 101), (B,), 0, 16)
    levels = jnp.array([0.0] * 11 + [8.0, 9.0, 10.0, 11.0, 12.0], jnp.float32)
    strength = jnp.sum(jnp.where(choose_level[:, None] == jnp.arange(16)[None, :], levels[None, :], 0.0), axis=1)
    sign_values = jax.random.randint(jax.random.fold_in(key, 102), (B, KVH, HD), 0, 2).astype(jnp.float32) * 2.0 - 1.0
    low_band = jnp.arange(HD) % (HD // 2) >= HD // 4
    direction = jnp.where(low_band[None, None, :], sign_values, 0.0)
    return (strength, direction)


def draw_context_hidden(key, part):
    key = jax.random.fold_in(key, 7)
    row_key, column_key, entry_key = jax.random.split(key, 3)
    row_scale = jnp.exp(jax.random.uniform(row_key, (B, CAP, 1), jnp.float32, 0.0, math.log(10.0)))
    column_scale = jnp.exp(jax.random.uniform(column_key, (1, 1, D), jnp.float32, 0.0, math.log(10.0)))
    random_base = jnp.clip(jax.random.normal(entry_key, (B, CAP, D), jnp.float32), -4.0, 4.0)
    return (0.05 * random_base * row_scale * column_scale).astype(jnp.bfloat16)


def draw_queries(key, part):
    strength, direction = strong_rows(key)
    key = jax.random.fold_in(key, 3)
    random_base = jnp.clip(jax.random.normal(key, (STEPS, B, HQ, HD), jnp.float32), -4.0, 4.0)
    aligned = jnp.repeat(direction, HQ // KVH, axis=1)[None] * strength[None, :, None, None]
    chosen = (strength > 0.0)[None, :, None, None]
    drawn = jnp.where(chosen, aligned, random_base)
    return drawn.reshape(STEPS, B, HQ * HD).astype(jnp.bfloat16)


def draw_new_kv(key, part):
    strength, direction = strong_rows(key)
    key = jax.random.fold_in(key, 4)
    random_base = jnp.clip(jax.random.normal(key, (2, STEPS, B, KVH, HD), jnp.float32), -4.0, 4.0)
    band_index = jnp.arange(HD) % (HD // 2) - HD // 4
    lowered = (band_index[None, :] < jnp.arange(STEPS)[:, None] * max(1, HD // 64)).astype(jnp.float32)
    level = strength[None, :, None] - lowered[:, None, :]
    aligned = level[:, :, None, :] * direction[None]
    key_part = jnp.where((strength > 0.0)[None, :, None, None], aligned, random_base[0])
    drawn = jnp.stack([key_part, random_base[1]])
    return drawn.reshape(2, STEPS, B, KVH * HD).astype(jnp.bfloat16)


def plant(values, rng, smallest, high):
    extent = values.shape
    spot = [jax.random.randint(jax.random.fold_in(rng, axis), (), 0, extent[axis]) for axis in range(len(extent))]
    values = values.at[tuple(spot)].set(smallest)
    longest = extent.index(max(extent))
    spot[longest] = (spot[longest] + 1) % extent[longest]
    return values.at[tuple(spot)].set(high)


def level_of(own_key, shape, shards, smallest, largest):
    gain, own = 1.0, jax.random.fold_in(own_key, 6)
    for axis_at, parts in shards:
        steps = jnp.exp(jax.random.uniform(jax.random.fold_in(own, axis_at), (parts,), jnp.float32, smallest / len(shards), largest / len(shards)))
        gain = gain * jnp.repeat(steps, shape[axis_at] // parts).reshape([-1 if axis == axis_at else 1 for axis in range(len(shape))])
    return gain


def length_profile(number_of, total, limit, lean):
    weights = [(1 << 20) // math.isqrt(standing ** lean) + 1 for standing in range(2, number_of + 1)]
    rest, holding = total - limit - (number_of - 1), [1] * (number_of - 1)
    while rest > 0:
        movable = [i for i in range(number_of - 1) if holding[i] < limit]
        pool, left = sum([weights[i] for i in movable]), rest
        for i in movable:
            more = min(limit - holding[i], max(1, left * weights[i] // pool), rest)
            holding[i] = holding[i] + more
            rest = rest - more
    return np.array([limit] + holding)


def uneven_parts(key, number_of, total, limit, skew):
    if number_of == 2:
        one = jax.random.randint(key, (), max(1, total - limit), min(limit, total - 1) + 1)
        return jnp.stack([one, total - one])
    sizes = jnp.asarray(length_profile(number_of, total, limit, skew), jnp.int32)
    twos = (number_of - 1) // 2
    donor, taker = sizes[1:1 + 2 * twos:2], sizes[2:2 + 2 * twos:2]
    room = jnp.minimum(donor - 1, limit - taker)
    shifted = jax.random.randint(jax.random.fold_in(key, 1), (twos,), 0, 1 << 20) % (room + 1)
    sizes = sizes.at[1:1 + 2 * twos:2].set(donor - shifted).at[2:2 + 2 * twos:2].set(taker + shifted)
    return sizes[jax.random.permutation(jax.random.fold_in(key, 2), number_of)]


def noise(own_key, shape, spread, most, shards=(), kind=jnp.bfloat16):
    values = spread * jax.random.normal(own_key, shape, jnp.float32)
    if shards:
        values = values * level_of(own_key, shape, shards, -0.22, 0.18)
    return jnp.clip(values, -most, most).astype(kind)


def setup_inputs(seed: int = 0) -> dict:
    keys = jax.random.split(jax.random.key(seed), 8)
    return {
        "context_hidden": draw_context_hidden(jax.random.fold_in(keys[7], 71), 0),
        "norm_gain": jnp.clip(1.0 + 0.15 * jax.random.normal(keys[1], (D,), jnp.float32), 0.25, 1.75),
        "kv_weight": noise(keys[2], (2, D, KVH * HD), D ** -0.5, 0.0625, ((1, 16), (2, 8))),
        "queries": draw_queries(jax.random.fold_in(keys[7], 71), 0),
        "new_kv": draw_new_kv(jax.random.fold_in(keys[7], 71), 0),
        "lengths": uneven_parts(keys[5], B, B * CAP // 2, CAP, 2).astype(jnp.int32),
        "slab_start": plant(jax.random.randint(keys[6], (B,), 0, 131072 - CAP - STEPS), jax.random.fold_in(keys[6], 1), 0, (131072 - CAP - STEPS) - 1).astype(jnp.int32),
    }


def rope_freqs():
    indices = jnp.arange(HD // 2, dtype=jnp.float32)
    base_freq = jnp.exp(-2.0 * indices / HD * math.log(500000.0))
    wavelength = 2.0 * math.pi / base_freq
    blend_weight = (8192.0 / wavelength - 1.0) / 3.0
    middle = (1.0 - blend_weight) * base_freq / 8.0 + blend_weight * base_freq
    return jnp.where(wavelength > 8192.0, base_freq / 8.0, jnp.where(wavelength < 2048.0, base_freq, middle))

def rotate(vectors, position, freqs):
    angles = position.astype(jnp.float32)[..., None, None] * freqs
    half_width = vectors.shape[-1] // 2
    first_half = vectors[..., :half_width]
    second = vectors[..., half_width:]
    cosine = jnp.cos(angles)
    sine_part = jnp.sin(angles)
    return jnp.concatenate([first_half * cosine - second * sine_part, second * cosine + first_half * sine_part], axis=-1)

def normalize(hidden, norm_gain):
    widened = hidden.astype(jnp.float32)
    rescale = lax.rsqrt(lax.optimization_barrier(jnp.mean(widened * widened, axis=-1, keepdims=True)) + 1e-05)
    return (widened * rescale * norm_gain).astype(jnp.bfloat16)

def reference(context_hidden, norm_gain, kv_weight, queries, new_kv, lengths, slab_start):
    freqs = rope_freqs()

    def restore(row_item):
        hidden, slab_offset = row_item
        normed = normalize(hidden, norm_gain)
        key_rows = jnp.dot(normed, kv_weight[0], preferred_element_type=jnp.float32)
        value_rows = jnp.dot(normed, kv_weight[1], preferred_element_type=jnp.float32)
        position = slab_offset + jnp.arange(CAP, dtype=jnp.int32)
        rotated = rotate(key_rows.reshape(CAP, KVH, HD), position, freqs).reshape(CAP, KVH * HD)
        return (rotated.astype(jnp.bfloat16), value_rows.astype(jnp.bfloat16))
    k_cache, v_cache = lax.map(restore, (context_hidden, slab_start))
    k_cache, v_cache = lax.optimization_barrier((k_cache, v_cache))
    group_size = HQ // KVH
    step_pos = (slab_start + lengths)[None, :] + jnp.arange(STEPS, dtype=jnp.int32)[:, None]
    rotated_query = rotate(queries.astype(jnp.float32).reshape(STEPS, B, HQ, HD), step_pos, freqs)
    rotated_query = rotated_query.reshape(STEPS, B, KVH, group_size, HD)
    fresh_keys = rotate(new_kv[0].astype(jnp.float32).reshape(STEPS, B, KVH, HD), step_pos, freqs)
    fresh_values = new_kv[1].astype(jnp.float32).reshape(STEPS, B, KVH, HD)
    cache_keys = k_cache.astype(jnp.float32).reshape(B, CAP, KVH, HD)
    cache_values = v_cache.astype(jnp.float32).reshape(B, CAP, KVH, HD)
    factor = 1.0 / math.sqrt(HD)
    cache_scores = jnp.einsum('ibgrd,bpgd->ibgrp', rotated_query, cache_keys) * factor
    fresh_scores = jnp.einsum('ibgrd,jbgd->ibgrj', rotated_query, fresh_keys) * factor
    live_mask = (jnp.arange(CAP, dtype=jnp.int32)[None, :] < lengths[:, None])[None, :, None, None, :]
    steps_index = jnp.arange(STEPS, dtype=jnp.int32)
    causal = (steps_index[None, :] <= steps_index[:, None])[:, None, None, None, :]
    cache_scores = jnp.where(live_mask, cache_scores, -1e+30)
    fresh_scores = jnp.where(causal, fresh_scores, -1e+30)
    peak_score = jnp.maximum(cache_scores.max(-1), fresh_scores.max(-1))[..., None]
    cache_weights = jnp.where(live_mask, jnp.exp(cache_scores - peak_score), 0.0)
    fresh_weights = jnp.where(causal, jnp.exp(fresh_scores - peak_score), 0.0)
    weight_sum = cache_weights.sum(-1) + fresh_weights.sum(-1)
    mixture = jnp.einsum('ibgrp,bpgd->ibgrd', cache_weights, cache_values)
    mixture = mixture + jnp.einsum('ibgrj,jbgd->ibgrd', fresh_weights, fresh_values)
    attention = (mixture / weight_sum[..., None]).reshape(STEPS, B, HQ * HD).astype(jnp.bfloat16)
    return (k_cache, v_cache, attention)
```

```python
import functools
import math

import jax
import jax.numpy as jnp
from jax import lax
from jax.experimental import pallas as pl
from jax.experimental.pallas import tpu as pltpu
from jax.sharding import PartitionSpec as P

HQ = 64
KVH = 8
HD = 128
STEPS = 4
B = 32
GROUP = HQ // KVH
ROWS = STEPS * GROUP
AXES = ("seq", "head")
X, Y, Z = 0, 1, 2
MIB = 1024 * 1024
VMEM = pl.BlockSpec(memory_space=pltpu.VMEM)
SMEM = pl.BlockSpec(memory_space=pltpu.SMEM)

PARTS = {"a": (192, (Y, Z, X)), "b": (192, (Z, X, Y)), "c": (128, (X, Y, Z))}


def place(n):
    s, h = n >> 3, n & 7
    return [h >> 1, (h & 1) * 2 + ((s >> 1) & 1), s >> 2, s & 1]


def flat(x, y, z, core):
    return (((z * 2 + (y & 1)) * 2 + core) * 4 + x) * 2 + (y >> 1)


def exchange(dim, step):
    pairs = []
    for n in range(128):
        spot = place(n)
        spot[dim] ^= (1, 3)[spot[3] ^ step]
        pairs.append((flat(*spot), n))
    return pairs


def siblings():
    return [(n, flat(*place(n)[:3], 1 - place(n)[3])) for n in range(128)]


def swap(value, dim, step):
    return lax.ppermute(value, AXES, exchange(dim, step))


def doubled(block, dim):
    pair = jnp.stack([block, swap(block, dim, 0)])
    return jnp.concatenate([pair, swap(pair, dim, 1)])


def rope_freqs():
    indices = jnp.arange(HD // 2, dtype=jnp.float32)
    base_freq = jnp.exp(-2.0 * indices / HD * math.log(500000.0))
    wavelength = 2.0 * math.pi / base_freq
    blend_weight = (8192.0 / wavelength - 1.0) / 3.0
    middle = (1.0 - blend_weight) * base_freq / 8.0 + blend_weight * base_freq
    return jnp.where(
        wavelength > 8192.0, base_freq / 8.0, jnp.where(wavelength < 2048.0, base_freq, middle)
    )


def tables(position, freqs):
    angles = position.astype(jnp.float32)[..., None] * freqs
    cosine, sine = jnp.cos(angles), jnp.sin(angles)
    return jnp.concatenate([cosine, cosine], -1), jnp.concatenate([-sine, sine], -1)


def rotated(vectors, cosine, sine):
    half = HD // 2
    swapped = jnp.concatenate([vectors[..., half:], vectors[..., :half]], -1)
    return vectors * cosine + swapped * sine


def prep_kernel(spot, even, odd, gain_even, gain_odd, own, send, scale, total):
    step = pl.program_id(0)
    core = spot[3]

    @pl.when(step == 0)
    def _():
        total[...] = jnp.zeros_like(total)

    x_even = even[...].astype(jnp.float32)
    x_odd = odd[...].astype(jnp.float32)
    squares = x_even * x_even + x_odd * x_odd
    total[...] += sum(squares[:, 128 * i : 128 * i + 128] for i in range(8))
    g_even = (x_even * gain_even[...]).astype(jnp.bfloat16)
    g_odd = (x_odd * gain_odd[...]).astype(jnp.bfloat16)
    lower = lax.broadcasted_iota(jnp.int32, (256, 128), 1) < 64
    ylo, zh = step // 2, step % 2
    tiles = []
    for parity in range(2):
        e = [g_even[:, 512 * parity + 128 * i : 512 * parity + 128 * i + 128] for i in range(4)]
        o = [g_odd[:, 512 * parity + 128 * i : 512 * parity + 128 * i + 128] for i in range(4)]
        tiles.append(
            (
                jnp.concatenate([e[0], jnp.where(lower, e[1], o[2]), o[3]], 1),
                jnp.concatenate([o[1], jnp.where(lower, o[2], e[1]), e[2]], 1),
                e[3],
                o[0],
            )
        )
    spots = (step * 384, 1536 + step * 384, 3072 + (4 * zh + ylo) * 128, 3072 + (4 * zh + 2 + ylo) * 128)
    for at, zero, one in zip(spots, *tiles):
        lanes = pl.ds(pl.multiple_of(at, 128), zero.shape[1])

        @pl.when(core == 0)
        def _():
            own[:, lanes] = zero
            send[:, lanes] = one

        @pl.when(core == 1)
        def _():
            own[:, lanes] = one
            send[:, lanes] = zero

    @pl.when(step == 3)
    def _():
        mean = jnp.sum(total[...], axis=1, keepdims=True) / 8192.0
        scale[...] = jnp.broadcast_to(lax.rsqrt(mean + 1e-05), (256, 128))


def prep(spot, hidden, gain):
    even = lambda step, spot: (0, 4 * (step % 2) + step // 2)
    odd = lambda step, spot: (0, 4 * (step % 2) + 2 + step // 2)
    whole = lambda step, spot: (0, 0)
    return pl.pallas_call(
        prep_kernel,
        out_shape=(
            jax.ShapeDtypeStruct((256, 4096), jnp.bfloat16),
            jax.ShapeDtypeStruct((256, 4096), jnp.bfloat16),
            jax.ShapeDtypeStruct((256, 128), jnp.float32),
        ),
        grid_spec=pltpu.PrefetchScalarGridSpec(
            num_scalar_prefetch=1,
            grid=(4,),
            in_specs=[
                pl.BlockSpec((256, 1024), even),
                pl.BlockSpec((256, 1024), odd),
                pl.BlockSpec((1, 1024), even),
                pl.BlockSpec((1, 1024), odd),
            ],
            out_specs=[
                pl.BlockSpec((256, 4096), whole),
                pl.BlockSpec((256, 4096), whole),
                pl.BlockSpec((256, 128), whole),
            ],
            scratch_shapes=[pltpu.VMEM((256, 128), jnp.float32)],
        ),
        compiler_params=pltpu.CompilerParams(vmem_limit_bytes=20 * MIB),
        cost_estimate=pl.CostEstimate(flops=8_000_000, bytes_accessed=8 * MIB, transcendentals=0),
    )(spot, hidden, hidden, gain, gain)


def product_kernel(slots, inputs, carried, narrow, spot, *refs):
    x_refs = refs[:inputs]
    piece_refs = refs[inputs : inputs + 3]
    if not carried:
        groups = list(zip("abc", piece_refs))
        rest = refs[inputs + 3 :]
    else:
        groups = list(zip("abc", piece_refs))
        rest = refs[inputs + 3 + inputs :]
        before = refs[inputs + 3 : inputs + 3 + inputs]
    outs, sums = rest[:inputs], rest[inputs:]
    mine = [spot[0], spot[1], spot[2]]
    core = spot[3]
    flips = [0, 1 + 2 * core, 3 - 2 * core, 2]

    def slot_of(flip):
        return jnp.where(flip == 0, 0, jnp.where(flip == flips[1], 1, jnp.where(flip == flips[2], 2, 3)))

    def at(dim, slot):
        return mine[dim] ^ flips[slot]

    for i in range(inputs):
        sums[i][...] = before[i][...] if carried else jnp.zeros_like(sums[i])

    def add(x_at, depth, weight, heads):
        for x_ref, total in zip(x_refs, sums):
            left = x_ref[:, pl.ds(pl.multiple_of(x_at, 128), depth)]
            result = jnp.dot(left, weight, preferred_element_type=jnp.float32)
            for i, head in enumerate(heads):
                total[head] += result[:, 128 * i : 128 * i + 128]

    z_slots = [slot_of(z ^ mine[Z]) for z in range(4)]
    y_slots = [slot_of(y ^ mine[Y]) for y in range(4)]
    for part, ref in groups:
        for index, slot in enumerate(slots):
            if part == "a":
                x = at(X, slot)
                for first, second in ((0, 3), (1, 2)):
                    y0, y1 = at(Y, first), at(Y, second)
                    weight = jnp.concatenate(
                        [
                            jnp.concatenate([ref[index, s, first], ref[index, s, second]], 1)
                            for s in z_slots
                        ],
                        0,
                    )
                    add(768 * (y0 & 1), 768, weight, [2 * x + (y0 >> 1), 2 * x + (y1 >> 1)])
            elif part == "b":
                y = at(Y, slot)
                weight = jnp.concatenate(
                    [
                        jnp.concatenate([ref[index, xs, z_slots[z]] for xs in range(4)], 1)
                        for z in (1, 0, 3, 2)
                    ],
                    0,
                )
                add(1536 + 768 * (y & 1), 768, weight, [2 * at(X, xs) + (y >> 1) for xs in range(4)])
            else:
                z = at(Z, slot)
                for yhi in range(2):
                    weight = jnp.concatenate(
                        [
                            jnp.concatenate([ref[index, y_slots[2 * yhi + ylo], xs] for xs in range(4)], 1)
                            for ylo in range(2)
                        ],
                        0,
                    )
                    add(3072 + 256 * z, 256, weight, [2 * at(X, xs) + yhi for xs in range(4)])
    if narrow:
        for i in range(inputs):
            outs[i][...] = sums[i][...].astype(outs[i].dtype)


def product(spot, rows, pieces, slots, before=None, narrow=False):
    carried = before is not None
    kind = jnp.bfloat16 if narrow else jnp.float32
    shape = (KVH, 256, HD)
    count = len(rows)

    def body(*refs):
        if narrow:
            product_kernel(slots, count, carried, True, *refs)
        else:
            product_kernel(slots, count, carried, False, *refs, *refs[-count:])

    return pl.pallas_call(
        body,
        out_shape=[jax.ShapeDtypeStruct(shape, kind)] * count,
        in_specs=[SMEM] + [VMEM] * (count + 3 + (count if carried else 0)),
        out_specs=[VMEM] * count,
        scratch_shapes=[pltpu.VMEM(shape, jnp.float32)] * (count if narrow else 0),
        compiler_params=pltpu.CompilerParams(vmem_limit_bytes=40 * MIB),
        cost_estimate=pl.CostEstimate(
            flops=count * len(slots) * 2 * 256 * 4096 * 256, bytes_accessed=4 * MIB, transcendentals=0
        ),
    )(spot, *rows, *pieces, *(before or ()))


def finish_kernel(keys, own, other, scale, *refs):
    out = refs[-1]
    for head in range(KVH):
        value = (own[head] + other[head].astype(jnp.float32)) * scale[...]
        if keys:
            value = value * refs[0][...] + pltpu.roll(value, HD // 2, 1) * refs[1][...]
        out[head] = value.astype(jnp.bfloat16)


def finish(own, other, scale, angles=()):
    return pl.pallas_call(
        functools.partial(finish_kernel, bool(angles)),
        out_shape=jax.ShapeDtypeStruct((KVH, 256, HD), jnp.bfloat16),
        in_specs=[VMEM] * (3 + len(angles)),
        out_specs=VMEM,
        compiler_params=pltpu.CompilerParams(vmem_limit_bytes=16 * MIB),
        cost_estimate=pl.CostEstimate(flops=2_000_000, bytes_accessed=3 * MIB, transcendentals=0),
    )(own, other, scale, *angles)


def cache_of(received):
    blocks = [received[i].astype(jnp.float32).reshape(B, 8, HD) for i in range(8)]
    return jnp.stack(blocks, axis=1).reshape(B, 64, HD)


def split(value):
    high = value.astype(jnp.bfloat16)
    return high, (value - high.astype(jnp.float32)).astype(jnp.bfloat16)


NT = (((1,), (1,)), ((), ()))


def score_kernel(spot, lengths, received, query, fresh, cache, weights, fresh_weights, marks):
    seq = spot[4]
    cache[...] = cache_of(received).astype(jnp.bfloat16)
    column = lax.broadcasted_iota(jnp.int32, (ROWS, 64), 1) + seq * 64
    late = lax.broadcasted_iota(jnp.int32, (ROWS, 8), 1)
    token = lax.broadcasted_iota(jnp.int32, (ROWS, 8), 0) // GROUP
    causal = late <= token
    diagonal = lax.broadcasted_iota(jnp.int32, (2 * ROWS, 128), 0)
    lane = lax.broadcasted_iota(jnp.int32, (2 * ROWS, 128), 1)
    factor = 1.0 / math.sqrt(HD)
    for pair in range(B // 2):
        peaks, sums = [], []
        for b in (2 * pair, 2 * pair + 1):
            high, low = split(query[b])
            both = lax.dot_general(
                jnp.concatenate([high, low], 0), cache[b], NT, preferred_element_type=jnp.float32
            )
            score = (both[:ROWS] + both[ROWS:]) * factor
            late_score = (
                lax.dot_general(
                    query[b], fresh[b], NT, preferred_element_type=jnp.float32, precision=lax.Precision.HIGHEST
                )
                * factor
            )
            live = column < lengths[b]
            new = causal & (seq == pair)
            score = jnp.where(live, score, -1e30)
            late_score = jnp.where(new, late_score, -1e30)
            peak = jnp.maximum(
                jnp.max(score, axis=1, keepdims=True), jnp.max(late_score, axis=1, keepdims=True)
            )
            weight = jnp.where(live, jnp.exp(score - peak), 0.0)
            late_weight = jnp.where(new, jnp.exp(late_score - peak), 0.0)
            weights[b] = weight
            fresh_weights[b] = late_weight
            peaks.append(peak)
            sums.append(jnp.sum(weight, axis=1, keepdims=True) + jnp.sum(late_weight, axis=1, keepdims=True))
        peak, total = jnp.concatenate(peaks, 0), jnp.concatenate(sums, 0)
        line = jnp.where(diagonal == lane, peak, 0.0) + jnp.where(diagonal + 64 == lane, total, 0.0)
        marks[pair] = jnp.broadcast_to(jnp.sum(line, axis=0, keepdims=True), (8, 128))


def score(spot, lengths, received, query, fresh):
    return pl.pallas_call(
        score_kernel,
        out_shape=(
            jax.ShapeDtypeStruct((B, 64, HD), jnp.bfloat16),
            jax.ShapeDtypeStruct((B, ROWS, 64), jnp.float32),
            jax.ShapeDtypeStruct((B, ROWS, 8), jnp.float32),
            jax.ShapeDtypeStruct((B // 2, 8, 128), jnp.float32),
        ),
        in_specs=[SMEM, SMEM, VMEM, VMEM, VMEM],
        out_specs=[VMEM] * 4,
        compiler_params=pltpu.CompilerParams(vmem_limit_bytes=16 * MIB),
        cost_estimate=pl.CostEstimate(flops=60_000_000, bytes_accessed=4 * MIB, transcendentals=70_000),
    )(spot, lengths, received, query, fresh)


def mix_kernel(received, weights, fresh_weights, fresh, marks, cache, packed):
    cache[...] = cache_of(received).astype(jnp.bfloat16)
    for b in range(B):
        high, low = split(weights[b])
        both = jnp.dot(jnp.concatenate([high, low], 0), cache[b], preferred_element_type=jnp.float32)
        high, low = split(fresh_weights[b])
        late = jnp.dot(jnp.concatenate([high, low], 0), fresh[b], preferred_element_type=jnp.float32)
        packed[b // 2, pl.ds(ROWS * (b % 2), ROWS)] = both[:ROWS] + both[ROWS:] + late[:ROWS] + late[ROWS:]
    packed[:, pl.ds(64, 8)] = marks[...]


def mix(received, weights, fresh_weights, fresh, marks):
    return pl.pallas_call(
        mix_kernel,
        out_shape=(
            jax.ShapeDtypeStruct((B, 64, HD), jnp.bfloat16),
            jax.ShapeDtypeStruct((B // 2, 72, HD), jnp.float32),
        ),
        in_specs=[VMEM] * 5,
        out_specs=[VMEM] * 2,
        compiler_params=pltpu.CompilerParams(vmem_limit_bytes=16 * MIB),
        cost_estimate=pl.CostEstimate(flops=60_000_000, bytes_accessed=4 * MIB, transcendentals=0),
    )(received, weights, fresh_weights, fresh, marks)


def merge_kernel(parts, out):
    marks = parts[:, 64]
    lane = lax.broadcasted_iota(jnp.int32, (16, 128), 1)
    peak = jnp.max(marks, axis=0, keepdims=True)
    grow = jnp.where(lane < 64, jnp.exp(marks - peak), 0.0)
    total = jnp.sum(grow * pltpu.roll(marks, 64, 1), axis=0, keepdims=True)
    share = grow / jnp.where(lane[:1] < 64, total, 1.0)
    columns = jnp.concatenate([share, jnp.zeros((112, 128), jnp.float32)], 0).T
    result = sum(parts[i, :64] * columns[:64, i : i + 1] for i in range(16))
    for b in range(2):
        for i in range(STEPS):
            out[i, b] = result[ROWS * b + GROUP * i : ROWS * b + GROUP * i + GROUP]


def merge(parts):
    return pl.pallas_call(
        merge_kernel,
        out_shape=jax.ShapeDtypeStruct((STEPS, 2, GROUP, HD), jnp.float32),
        in_specs=[VMEM],
        out_specs=VMEM,
        cost_estimate=pl.CostEstimate(flops=300_000, bytes_accessed=MIB, transcendentals=2048),
    )(parts)


def shards(context_hidden, norm_gain, kv_weight, queries, new_kv, lengths, slab_start):
    seq, head = lax.axis_index("seq"), lax.axis_index("head")
    z, ylo, core = seq >> 2, (seq >> 1) & 1, seq & 1
    x, yhi = head >> 1, head & 1
    spot = jnp.stack([x, yhi * 2 + ylo, z, core, seq]).astype(jnp.int32)
    odd = z & 1
    starts = {
        "a": jnp.where(odd, 320, 0),
        "b": jnp.where(odd, 128, 192),
        "c": jnp.where(odd, 0, 384),
    }

    first = {
        part: doubled(lax.dynamic_slice_in_dim(kv_weight, starts[part], depth, 1), dims[0])
        for part, (depth, dims) in PARTS.items()
    }

    own_rows, sent_rows, scale = prep(spot, context_hidden.reshape(256, 8192), norm_gain.reshape(1, 8192))
    other_rows = lax.ppermute(sent_rows, AXES, siblings())

    freqs = rope_freqs()
    position = (
        slab_start[:, None] + (seq * 8 + head) * 8 + jnp.arange(8, dtype=jnp.int32)[None, :]
    ).reshape(256)
    angles = tables(position, freqs)
    step_pos = (slab_start + lengths)[:, None] + jnp.arange(STEPS, dtype=jnp.int32)[None, :]
    step_cos, step_sin = tables(step_pos, freqs)
    query = queries.astype(jnp.float32).reshape(STEPS, B, GROUP, HD).transpose(1, 0, 2, 3)
    query = rotated(query, step_cos[:, :, None], step_sin[:, :, None]).reshape(B, ROWS, HD)
    fresh = new_kv.astype(jnp.float32).transpose(0, 2, 1, 3)
    padding = ((0, 0), (0, 8 - STEPS), (0, 0))
    fresh_keys = jnp.pad(rotated(fresh[0], step_cos, step_sin), padding)
    fresh_values = jnp.pad(new_kv[1].transpose(1, 0, 2), padding)

    finished = []
    for kind in range(2):
        near, far = [], []
        for part, (depth, dims) in PARTS.items():
            block = doubled(first[part][:, kind], dims[1])
            pair = jnp.stack([block, swap(block, dims[2], 0)])
            near.append(pair)
            far.append(swap(pair, dims[2], 1))
        own, other = product(spot, [own_rows, other_rows], near, (0, 1))
        (other,) = product(spot, [other_rows], far, (2, 3), [other], narrow=True)
        (own,) = product(spot, [own_rows], far, (2, 3), [own])
        arrived = lax.ppermute(other, AXES, siblings())
        rows = finish(own, arrived, scale, angles if kind == 0 else ())
        received = lax.all_to_all(rows, "head", 0, 0)
        if kind == 0:
            k_cache, weights, late, marks = score(spot, lengths, received, query, fresh_keys)
        else:
            v_cache, packed = mix(received, weights, late, fresh_values, marks)
    parts = lax.all_to_all(packed, "seq", 0, 0)
    attention = merge(parts).astype(jnp.bfloat16).reshape(STEPS, 2, GROUP * HD)
    return k_cache, v_cache, attention


def solution(mesh):
    return jax.shard_map(
        shards,
        mesh=mesh,
        in_specs=(
            P(None, ("seq", "head"), None),
            P(),
            P(None, "seq", "head"),
            P(None, None, "head"),
            P(None, None, None, "head"),
            P(),
            P(),
        ),
        out_specs=(P(None, "seq", "head"), P(None, "seq", "head"), P(None, "seq", "head")),
        check_vma=False,
    )
```

```python
import functools
import math

import jax
import jax.numpy as jnp
from jax import lax
from jax.experimental import pallas as pl
from jax.experimental.pallas import tpu as pltpu
from jax.sharding import Mesh
from jax.sharding import PartitionSpec as P

HQ = 64
KVH = 8
HD = 128
STEPS = 4
B = 32
GROUP = HQ // KVH
ROWS = STEPS * GROUP
AXES = ("z", "ylo", "core", "x", "yhi")
SEQ, HEAD = AXES[:3], AXES[3:]
X, Y, Z = 0, 1, 2
MIB = 1024 * 1024
LIMIT = 8
VMEM = pl.BlockSpec(memory_space=pltpu.VMEM)
SMEM = pl.BlockSpec(memory_space=pltpu.SMEM)

HALF = 256


def place(n):
    s, h = n >> 3, n & 7
    return [h >> 1, (h & 1) * 2 + ((s >> 1) & 1), s >> 2, s & 1]


def flat(x, y, z, core):
    return (((z * 2 + (y & 1)) * 2 + core) * 4 + x) * 2 + (y >> 1)


def exchange(dim, step):
    pairs = []
    for n in range(128):
        spot = place(n)
        spot[dim] ^= (1, 3)[spot[3] ^ step]
        pairs.append((flat(*spot), n))
    return pairs


def flipped(x=0, y=0, core=0):
    pairs = []
    for n in range(128):
        spot = place(n)
        pairs.append((flat(spot[0] ^ x, spot[1] ^ y, spot[2], spot[3] ^ core), n))
    return pairs


def swap(value, dim, step):
    return lax.ppermute(value, AXES, exchange(dim, step))


def together(*values):
    return lax.optimization_barrier(values)


def doubled(block, dim):
    pair = jnp.stack([block, swap(block, dim, 0)])
    return jnp.concatenate([pair, swap(pair, dim, 1)])


def rope_freqs():
    indices = jnp.arange(HD // 2, dtype=jnp.float32)
    base_freq = jnp.exp(-2.0 * indices / HD * math.log(500000.0))
    wavelength = 2.0 * math.pi / base_freq
    blend_weight = (8192.0 / wavelength - 1.0) / 3.0
    middle = (1.0 - blend_weight) * base_freq / 8.0 + blend_weight * base_freq
    return jnp.where(
        wavelength > 8192.0, base_freq / 8.0, jnp.where(wavelength < 2048.0, base_freq, middle)
    )


def tables(position, freqs):
    angles = position.astype(jnp.float32)[..., None] * freqs
    cosine, sine = jnp.cos(angles), jnp.sin(angles)
    return jnp.concatenate([cosine, cosine], -1), jnp.concatenate([-sine, sine], -1)


def rotated(vectors, cosine, sine):
    half = HD // 2
    swapped = jnp.concatenate([vectors[..., half:], vectors[..., :half]], -1)
    return vectors * cosine + swapped * sine


def prep_kernel(spot, hidden, gain, own, side, across, corner, total):
    step = pl.program_id(1)
    mine = 2 * (spot[1] & 1) + spot[3]
    x = hidden[...].astype(jnp.float32)

    @pl.when(pl.program_id(0) == 0)
    def _():
        squares = x * x
        part = sum(squares[:, 128 * i : 128 * i + 128] for i in range(16))

        @pl.when(step == 0)
        def _():
            total[...] = part

        @pl.when(step > 0)
        def _():
            total[...] += part

        @pl.when(step == 3)
        def _():
            mean = jnp.sum(total[...], axis=1, keepdims=True) / 8192.0
            total[...] = jnp.broadcast_to(lax.rsqrt(mean + 1e-05), (256, 128))

    @pl.when(pl.program_id(0) == 1)
    def _():
        normed = (x * total[:, :1] * gain[...]).astype(jnp.bfloat16)
        quarters = [normed[:, 512 * i : 512 * i + 512] for i in range(4)]
        for at in range(2):
            lanes = pl.ds(pl.multiple_of(1024 * at + HALF * step, HALF), HALF)
            blocks = [quarter[:, HALF * at : HALF * at + HALF] for quarter in quarters]
            for owner in range(4):

                @pl.when(mine == owner)
                def _():
                    own[:, lanes] = blocks[owner]
                    side[:, lanes] = blocks[owner ^ 1]
                    across[:, lanes] = blocks[owner ^ 2]
                    corner[:, lanes] = blocks[owner ^ 3]


def prep(spot, hidden, gain):
    block = lambda turn, step, spot: (0, step)
    whole = lambda turn, step, spot: (0, 0)
    return pl.pallas_call(
        prep_kernel,
        out_shape=(
            *[jax.ShapeDtypeStruct((256, 2048), jnp.bfloat16)] * 4,
        ),
        grid_spec=pltpu.PrefetchScalarGridSpec(
            num_scalar_prefetch=1,
            grid=(2, 4),
            in_specs=[pl.BlockSpec((256, 2048), block), pl.BlockSpec((1, 2048), block)],
            out_specs=[pl.BlockSpec((256, 2048), whole)] * 4,
            scratch_shapes=[pltpu.VMEM((256, 128), jnp.float32)],
        ),
        compiler_params=pltpu.CompilerParams(vmem_limit_bytes=20 * MIB),
        cost_estimate=pl.CostEstimate(flops=1_000_000, bytes_accessed=MIB // 4, transcendentals=0),
    )(spot, hidden, gain)


def product_kernel(slots, inputs, carried, narrow, spot, *refs):
    x_refs, refs = refs[:inputs], refs[inputs:]
    piece_refs, refs = refs[: 2 * len(slots)], refs[2 * len(slots) :]
    if carried:
        before, refs = refs[:inputs], refs[inputs:]
    if narrow:
        out, sums = refs[0], refs[1:]
    else:
        sums = refs
    mine = [spot[0], spot[1], spot[2]]
    core = spot[3]
    flips = [0, 1 + 2 * core, 3 - 2 * core, 2]

    def slot_of(flip):
        return jnp.where(flip == 0, 0, jnp.where(flip == flips[1], 1, jnp.where(flip == flips[2], 2, 3)))

    for i in range(inputs):
        sums[i][...] = before[i][...] if carried else jnp.zeros_like(sums[i])

    def add(x_at, depth, weight, heads):
        for x_ref, total in zip(x_refs, sums):
            left = x_ref[:, pl.ds(pl.multiple_of(x_at, HALF), depth)]
            result = jnp.dot(left, weight, preferred_element_type=jnp.float32)
            for i, (head, kind) in enumerate(heads):
                total[kind, head] += result[:, 128 * i : 128 * i + 128]

    z_slots = [slot_of(z ^ mine[Z]) for z in range(4)]
    yhi = [mine[Y] >> 1, 1 - (mine[Y] >> 1)]
    places = [(ys, kind) for ys in range(2) for kind in range(2)]
    for i, slot in enumerate(slots):
        ref = piece_refs[2 * i]
        x = mine[X] ^ flips[slot]
        weight = jnp.concatenate(
            [jnp.concatenate([ref[s, ys, kind] for ys, kind in places], 1) for s in z_slots], 0
        )
        add(0, 1024, weight, [(2 * x + yhi[ys], kind) for ys, kind in places])
        ref = piece_refs[2 * i + 1]
        z = mine[Z] ^ flips[slot]
        for xs in range(4):
            weight = jnp.concatenate([ref[xs, ys, kind] for ys, kind in places], 1)
            x = mine[X] ^ flips[xs]
            add(1024 + HALF * z, HALF, weight, [(2 * x + yhi[ys], kind) for ys, kind in places])
    if narrow:
        for i in range(inputs):
            out[i] = sums[i][...].astype(out.dtype)


def product(spot, rows, pieces, slots, before=None, narrow=False):
    carried = before is not None
    shape = (2, KVH, 256, HD)
    count = len(rows)
    if narrow:
        out_shape = [jax.ShapeDtypeStruct((count, *shape), jnp.bfloat16)]
    else:
        out_shape = [jax.ShapeDtypeStruct(shape, jnp.float32)] * count
    return pl.pallas_call(
        functools.partial(product_kernel, slots, count, carried, narrow),
        out_shape=out_shape,
        in_specs=[SMEM] + [VMEM] * (count + len(pieces) + (count if carried else 0)),
        out_specs=[VMEM] * len(out_shape),
        scratch_shapes=[pltpu.VMEM(shape, jnp.float32)] * (count if narrow else 0),
        compiler_params=pltpu.CompilerParams(vmem_limit_bytes=LIMIT * MIB),
        cost_estimate=pl.CostEstimate(flops=1_000_000, bytes_accessed=MIB // 4, transcendentals=0),
    )(spot, *rows, *pieces, *(before or ()))


def finish_kernel(spot, own, across, side, *refs):
    out = refs[-1]
    mine = spot[1] & 1
    for i, part in enumerate((own, across)):
        for kind in range(2):
            for head in range(KVH):
                value = part[kind, head] + side[i, kind, head].astype(jnp.float32)
                if kind == 0:
                    value = value * refs[2 * i][...] + pltpu.roll(value, HD // 2, 1) * refs[2 * i + 1][...]
                out[mine ^ i, head, kind] = value.astype(jnp.bfloat16)


def finish(spot, own, across, side, angles):
    out = pl.pallas_call(
        finish_kernel,
        out_shape=jax.ShapeDtypeStruct((2, KVH, 2, 256, HD), jnp.bfloat16),
        in_specs=[SMEM] + [VMEM] * (3 + len(angles)),
        out_specs=VMEM,
        compiler_params=pltpu.CompilerParams(vmem_limit_bytes=8 * MIB),
        cost_estimate=pl.CostEstimate(flops=4_000_000, bytes_accessed=MIB, transcendentals=0),
    )(spot, own, across, side, *angles)
    return out.reshape(16, 2, 256, HD)


def cache_of(received, kind):
    blocks = [
        (received[i, kind].astype(jnp.float32) + received[8 + i, kind].astype(jnp.float32)).reshape(B, 8, HD)
        for i in range(8)
    ]
    return jnp.stack(blocks, axis=1).reshape(B, 64, HD)


def split(value):
    high = value.astype(jnp.bfloat16)
    return high, (value - high.astype(jnp.float32)).astype(jnp.bfloat16)


NT = (((1,), (1,)), ((), ()))


def line_of(peak, total):
    row = lax.broadcasted_iota(jnp.int32, (2 * ROWS, 128), 0)
    lane = lax.broadcasted_iota(jnp.int32, (2 * ROWS, 128), 1)
    line = jnp.where(row == lane, peak, 0.0) + jnp.where(row + 64 == lane, total, 0.0)
    line = jnp.sum(line, axis=0, keepdims=True)
    high = line.astype(jnp.bfloat16).astype(jnp.float32)
    middle = (line - high).astype(jnp.bfloat16).astype(jnp.float32)
    at = lax.broadcasted_iota(jnp.int32, (16, 128), 0)
    terms = jnp.where(at == 0, high, jnp.where(at == 1, middle, line - high - middle))
    return jnp.where(at < 3, terms, 0.0).astype(jnp.bfloat16)


def scored(query, keys, length, column):
    both = lax.dot_general(jnp.concatenate(split(query), 0), keys, NT, preferred_element_type=jnp.float32)
    return jnp.where(column < length, (both[:ROWS] + both[ROWS:]) * (1.0 / math.sqrt(HD)), -1e30)


def weighted(weight, values):
    both = jnp.dot(jnp.concatenate(split(weight), 0), values, preferred_element_type=jnp.float32)
    return both[:ROWS] + both[ROWS:]


def attend_kernel(spot, lengths, received, query, fresh_keys, fresh_values, keys, values, packed, scores):
    seq = spot[4]
    keys[...] = cache_of(received, 0).astype(jnp.bfloat16)
    values[...] = cache_of(received, 1).astype(jnp.bfloat16)
    column = lax.broadcasted_iota(jnp.int32, (ROWS, 64), 1) + seq * 64
    for b in range(B):
        scores[pl.ds(ROWS * b, ROWS)] = scored(query[b], keys[b], lengths[b], column)
    score = scores[...]
    peak = jnp.max(score, axis=1, keepdims=True)
    weight = jnp.where(score > -1e29, jnp.exp(score - peak), 0.0)
    total = jnp.sum(weight, axis=1, keepdims=True)
    for b in range(B):
        mixed = weighted(weight[ROWS * b : ROWS * b + ROWS], values[b])
        packed[b // 2, pl.ds(ROWS * (b % 2), ROWS)] = mixed.astype(jnp.bfloat16)
    for pair in range(B // 2):
        rows = slice(2 * ROWS * pair, 2 * ROWS * pair + 2 * ROWS)
        packed[pair, pl.ds(64, 16)] = line_of(peak[rows], total[rows])

    late = lax.broadcasted_iota(jnp.int32, (ROWS, 8), 1)
    token = lax.broadcasted_iota(jnp.int32, (ROWS, 8), 0) // GROUP
    peaks, totals = [], []
    for i in range(2):
        b = 2 * seq + i
        score = scored(query[b], keys[b], lengths[b], column)
        late_score = (1.0 / math.sqrt(HD)) * lax.dot_general(
            query[b], fresh_keys[b], NT, preferred_element_type=jnp.float32, precision=lax.Precision.HIGHEST
        )
        late_score = jnp.where(late <= token, late_score, -1e30)
        peak = jnp.maximum(jnp.max(score, axis=1, keepdims=True), jnp.max(late_score, axis=1, keepdims=True))
        weight = jnp.where(score > -1e29, jnp.exp(score - peak), 0.0)
        late_weight = jnp.where(late <= token, jnp.exp(late_score - peak), 0.0)
        mixed = weighted(weight, values[b]) + weighted(late_weight, fresh_values[b])
        packed[seq, pl.ds(ROWS * i, ROWS)] = mixed.astype(jnp.bfloat16)
        peaks.append(peak)
        totals.append(jnp.sum(weight, axis=1, keepdims=True) + jnp.sum(late_weight, axis=1, keepdims=True))
    packed[seq, pl.ds(64, 16)] = line_of(jnp.concatenate(peaks, 0), jnp.concatenate(totals, 0))


def attend(spot, lengths, received, query, fresh_keys, fresh_values):
    return pl.pallas_call(
        attend_kernel,
        out_shape=(
            jax.ShapeDtypeStruct((B, 64, HD), jnp.bfloat16),
            jax.ShapeDtypeStruct((B, 64, HD), jnp.bfloat16),
            jax.ShapeDtypeStruct((B // 2, 80, HD), jnp.bfloat16),
        ),
        in_specs=[SMEM, SMEM] + [VMEM] * 4,
        out_specs=[VMEM] * 3,
        scratch_shapes=[pltpu.VMEM((B * ROWS, 64), jnp.float32)],
        compiler_params=pltpu.CompilerParams(vmem_limit_bytes=16 * MIB),
        cost_estimate=pl.CostEstimate(flops=60_000_000, bytes_accessed=4 * MIB, transcendentals=70_000),
    )(spot, lengths, received, query, fresh_keys, fresh_values)


def merge_kernel(parts, out):
    lines = [jnp.sum(parts[i, 64:80].astype(jnp.float32), axis=0, keepdims=True) for i in range(16)]
    marks = jnp.concatenate(lines, 0)
    lane = lax.broadcasted_iota(jnp.int32, (16, 128), 1)
    peak = jnp.max(marks, axis=0, keepdims=True)
    grow = jnp.where(lane < 64, jnp.exp(marks - peak), 0.0)
    total = jnp.sum(grow * pltpu.roll(marks, 64, 1), axis=0, keepdims=True)
    share = grow / jnp.where(lane[:1] < 64, total, 1.0)
    columns = jnp.concatenate([share, jnp.zeros((112, 128), jnp.float32)], 0).T
    result = sum(parts[i, :64].astype(jnp.float32) * columns[:64, i : i + 1] for i in range(16))
    for i in range(STEPS):
        rows = [
            jnp.concatenate(
                [result[at + r : at + r + 1] for r in range(GROUP)], 1
            )
            for at in (GROUP * i, ROWS + GROUP * i)
        ]
        out[i] = jnp.concatenate(rows, 0).astype(jnp.bfloat16)


def merge(parts):
    return pl.pallas_call(
        merge_kernel,
        out_shape=jax.ShapeDtypeStruct((STEPS, 2, GROUP * HD), jnp.bfloat16),
        in_specs=[VMEM],
        out_specs=VMEM,
        cost_estimate=pl.CostEstimate(flops=300_000, bytes_accessed=MIB, transcendentals=2048),
    )(parts)


def shards(context_hidden, norm_gain, kv_weight, queries, new_kv, lengths, slab_start):
    seq, head = lax.axis_index(SEQ), lax.axis_index(HEAD)
    z, ylo, core = seq >> 2, (seq >> 1) & 1, seq & 1
    x, yhi = head >> 1, head & 1
    spot = jnp.stack([x, yhi * 2 + ylo, z, core, seq]).astype(jnp.int32)

    weight = jnp.stack([kv_weight, lax.ppermute(kv_weight, AXES, flipped(y=2))])
    own_rows, to_side, to_across, to_corner = prep(
        spot, context_hidden.reshape(256, 8192), norm_gain.reshape(1, 8192)
    )
    weight, own_rows = together(weight, own_rows)
    corner_rows = lax.ppermute(to_corner, AXES, flipped(y=1))
    across_rows = lax.ppermute(to_across, AXES, flipped(y=1))
    side_rows = lax.ppermute(to_side, AXES, flipped(core=1))
    middle, last = (Z, X), (X, Z)
    halves = [weight[:, :, :HALF], weight[:, :, HALF:]]
    firsts = [swap(half, dim, 0) for half, dim in zip(halves, middle)]
    firsts = together(*firsts)
    pairs = [jnp.stack(pair) for pair in zip(halves, firsts)]
    seconds = [swap(pair, dim, 1) for pair, dim in zip(pairs, middle)]
    blocks = [jnp.concatenate(both) for both in zip(pairs, seconds)]
    blocks, side_rows, queries, new_kv, slab_start = together(blocks, side_rows, queries, new_kv, slab_start)

    one = [swap(block, dim, 0) for block, dim in zip(blocks, last)]
    two = [swap(block, dim, 1) for block, dim in zip(blocks, last)]
    one, two, corner_rows = together(one, two, corner_rows)
    far = [swap(block, dim, 1) for block, dim in zip(one, last)]
    corner_rows = lax.ppermute(corner_rows, AXES, flipped(core=1))

    freqs = rope_freqs()
    angles = ()
    for near in (seq, seq ^ 2):
        position = slab_start[:, None] + (near * 8 + head) * 8 + jnp.arange(8, dtype=jnp.int32)[None, :]
        angles += tables(position.reshape(256), freqs)
    step_pos = (slab_start + lengths)[:, None] + jnp.arange(STEPS, dtype=jnp.int32)[None, :]
    step_cos, step_sin = tables(step_pos, freqs)
    query = queries.astype(jnp.float32).reshape(STEPS, B, GROUP, HD).transpose(1, 0, 2, 3)
    query = rotated(query, step_cos[:, :, None], step_sin[:, :, None]).reshape(B, ROWS, HD)
    fresh = new_kv.astype(jnp.float32).transpose(0, 2, 1, 3)
    padding = ((0, 0), (0, 8 - STEPS), (0, 0))
    fresh_keys = jnp.pad(rotated(fresh[0], step_cos, step_sin), padding)
    fresh_values = jnp.pad(new_kv[1].transpose(1, 0, 2), padding)
    spot_ready, *_ = together(spot, query, fresh_keys, fresh_values, angles)

    near = [*blocks, *one, *two]
    own, side = product(spot_ready, [own_rows, side_rows], near, (0, 1, 2))
    spot_later, own, side = together(spot_ready, own, side)
    corner, across = product(spot_later, [corner_rows, across_rows], near, (0, 1, 2))
    (sent,) = product(spot, [side_rows, corner_rows], far, (3,), [side, corner], narrow=True)
    side = lax.ppermute(sent, AXES, flipped(core=1))
    own, across = product(spot, [own_rows, across_rows], far, (3,), [own, across])
    rows = finish(spot, own, across, side, angles)
    received = lax.all_to_all(rows, ("ylo", "x", "yhi"), 0, 0)
    k_cache, v_cache, packed = attend(spot, lengths, received, query, fresh_keys, fresh_values)
    parts = lax.all_to_all(packed, SEQ, 0, 0)
    attention = merge(parts)
    return k_cache, v_cache, attention


def solution(mesh):
    fine = Mesh(mesh.devices.reshape(4, 2, 2, 4, 2), AXES)
    return jax.shard_map(
        shards,
        mesh=fine,
        in_specs=(
            P(None, AXES, None),
            P(),
            P(None, SEQ, HEAD),
            P(None, None, HEAD),
            P(None, None, None, HEAD),
            P(),
            P(),
        ),
        out_specs=(P(None, SEQ, HEAD), P(None, SEQ, HEAD), P(None, SEQ, HEAD)),
        check_vma=False,
    )
```

```python
import functools
import math

import jax
import jax.numpy as jnp
from jax import lax
from jax.experimental import pallas as pl
from jax.experimental.pallas import tpu as pltpu
from jax.sharding import Mesh
from jax.sharding import PartitionSpec as P

HQ = 64
KVH = 8
HD = 128
STEPS = 4
B = 32
GROUP = HQ // KVH
ROWS = STEPS * GROUP
AXES = ("z", "ylo", "core", "x", "yhi")
SEQ, HEAD = AXES[:3], AXES[3:]
X, Y, Z = 0, 1, 2
MIB = 1024 * 1024
LIMIT = 8
VMEM = pl.BlockSpec(memory_space=pltpu.VMEM)
SMEM = pl.BlockSpec(memory_space=pltpu.SMEM)

HALF = 256


def place(n):
    s, h = n >> 3, n & 7
    return [h >> 1, (h & 1) * 2 + ((s >> 1) & 1), s >> 2, s & 1]


def flat(x, y, z, core):
    return (((z * 2 + (y & 1)) * 2 + core) * 4 + x) * 2 + (y >> 1)


def exchange(dim, step):
    pairs = []
    for n in range(128):
        spot = place(n)
        spot[dim] ^= (1, 3)[spot[3] ^ step]
        pairs.append((flat(*spot), n))
    return pairs


def flipped(x=0, y=0, core=0):
    pairs = []
    for n in range(128):
        spot = place(n)
        pairs.append((flat(spot[0] ^ x, spot[1] ^ y, spot[2], spot[3] ^ core), n))
    return pairs


def swap(value, dim, step):
    return lax.ppermute(value, AXES, exchange(dim, step))


def together(*values):
    return lax.optimization_barrier(values)


def doubled(block, dim):
    pair = jnp.stack([block, swap(block, dim, 0)])
    return jnp.concatenate([pair, swap(pair, dim, 1)])


def rope_freqs():
    indices = jnp.arange(HD // 2, dtype=jnp.float32)
    base_freq = jnp.exp(-2.0 * indices / HD * math.log(500000.0))
    wavelength = 2.0 * math.pi / base_freq
    blend_weight = (8192.0 / wavelength - 1.0) / 3.0
    middle = (1.0 - blend_weight) * base_freq / 8.0 + blend_weight * base_freq
    return jnp.where(
        wavelength > 8192.0, base_freq / 8.0, jnp.where(wavelength < 2048.0, base_freq, middle)
    )


def tables(position, freqs):
    angles = position.astype(jnp.float32)[..., None] * freqs
    cosine, sine = jnp.cos(angles), jnp.sin(angles)
    return jnp.concatenate([cosine, cosine], -1), jnp.concatenate([-sine, sine], -1)


def rotated(vectors, cosine, sine):
    half = HD // 2
    swapped = jnp.concatenate([vectors[..., half:], vectors[..., :half]], -1)
    return vectors * cosine + swapped * sine


def prep_kernel(spot, hidden, gain, own, side, across, corner, rows, total, sems):
    mine = 2 * (spot[1] & 1) + spot[3]
    copies = []
    for i in range(4):
        lanes = pl.ds(2048 * i, 2048)
        copies.append(pltpu.make_async_copy(hidden.at[:, lanes], rows.at[:, lanes], sems.at[i]))
        copies[i].start()
    for i in range(4):
        copies[i].wait()

        def add(tile, _, i=i):
            at = pl.ds(pl.multiple_of(16 * tile, 16), 16)
            part = 0.0 if i == 0 else total[at, :]
            for lane in range(2048 * i, 2048 * i + 2048, 128):
                x = rows[at, lane : lane + 128].astype(jnp.float32)
                part = part + x * x
            total[at, :] = part
            return 0

        lax.fori_loop(0, 16, add, 0)
    mean = jnp.sum(total[...], axis=1, keepdims=True) / 8192.0
    total[...] = jnp.broadcast_to(lax.rsqrt(mean + 1e-05), (256, 128))
    for owner in range(4):

        @pl.when(mine == owner)
        def _():
            outs = (own, side, across, corner)

            def write(tile, _):
                at = pl.ds(pl.multiple_of(16 * tile, 16), 16)
                scale = total[at, :]
                for lane in range(0, 8192, 128):
                    z, quarter, half, rest = lane // 2048, lane // 512 % 4, lane // HALF % 2, lane % HALF
                    x = rows[at, lane : lane + 128].astype(jnp.float32)
                    x = x * scale * gain[:, lane : lane + 128]
                    to = 1024 * half + HALF * z + rest
                    outs[quarter ^ owner][at, to : to + 128] = x.astype(jnp.bfloat16)
                return 0

            lax.fori_loop(0, 16, write, 0)


def prep(spot, hidden, gain):
    return pl.pallas_call(
        prep_kernel,
        out_shape=[jax.ShapeDtypeStruct((256, 2048), jnp.bfloat16)] * 4,
        in_specs=[SMEM, pl.BlockSpec(memory_space=pl.ANY), VMEM],
        out_specs=[VMEM] * 4,
        scratch_shapes=[
            pltpu.VMEM((256, 8192), jnp.bfloat16),
            pltpu.VMEM((256, 128), jnp.float32),
            pltpu.SemaphoreType.DMA((4,)),
        ],
        compiler_params=pltpu.CompilerParams(vmem_limit_bytes=48 * MIB),
        cost_estimate=pl.CostEstimate(flops=1_000_000, bytes_accessed=MIB // 4, transcendentals=0),
    )(spot, hidden, gain)


def product_kernel(slots, inputs, carried, narrow, spot, *refs):
    x_refs, refs = refs[:inputs], refs[inputs:]
    piece_refs, refs = refs[: 2 * len(slots)], refs[2 * len(slots) :]
    if carried:
        before, refs = refs[:inputs], refs[inputs:]
    if narrow:
        out = refs[0]
    else:
        sums = refs
    mine = [spot[0], spot[1], spot[2]]
    core = spot[3]
    flips = [0, 1 + 2 * core, 3 - 2 * core, 2]

    def slot_of(flip):
        return jnp.where(flip == 0, 0, jnp.where(flip == flips[1], 1, jnp.where(flip == flips[2], 2, 3)))

    z_slots = [slot_of(z ^ mine[Z]) for z in range(4)]
    yhi = [mine[Y] >> 1, 1 - (mine[Y] >> 1)]
    places = [(ys, kind) for ys in range(2) for kind in range(2)]
    for xs in range(4):
        lanes, weight = [], []
        for i, slot in enumerate(slots):
            ref = piece_refs[2 * i + 1]
            z = mine[Z] ^ flips[slot]
            lanes.append(pl.ds(pl.multiple_of(1024 + HALF * z, HALF), HALF))
            weight.append(jnp.concatenate([ref[xs, ys, kind] for ys, kind in places], 1))
            if slot == xs:
                ref = piece_refs[2 * i]
                lanes.append(pl.ds(0, 1024))
                weight += [jnp.concatenate([ref[s, ys, kind] for ys, kind in places], 1) for s in z_slots]
        weight = jnp.concatenate(weight, 0)
        x = mine[X] ^ flips[xs]
        left = jnp.concatenate([jnp.concatenate([rows[:, at] for rows in x_refs], 0) for at in lanes], 1)
        result = jnp.dot(left, weight, preferred_element_type=jnp.float32)
        for n in range(inputs):
            for i, (ys, kind) in enumerate(places):
                value = result[256 * n : 256 * n + 256, 128 * i : 128 * i + 128]
                if carried:
                    value = value + before[n][kind, 2 * x + yhi[ys]]
                if narrow:
                    out[n, kind, 2 * x + yhi[ys]] = value.astype(out.dtype)
                else:
                    sums[n][kind, 2 * x + yhi[ys]] = value


def product(spot, rows, pieces, slots, before=None, narrow=False):
    carried = before is not None
    shape = (2, KVH, 256, HD)
    count = len(rows)
    if narrow:
        out_shape = [jax.ShapeDtypeStruct((count, *shape), jnp.bfloat16)]
    else:
        out_shape = [jax.ShapeDtypeStruct(shape, jnp.float32)] * count
    return pl.pallas_call(
        functools.partial(product_kernel, slots, count, carried, narrow),
        out_shape=out_shape,
        in_specs=[SMEM] + [VMEM] * (count + len(pieces) + (count if carried else 0)),
        out_specs=[VMEM] * len(out_shape),
        compiler_params=pltpu.CompilerParams(vmem_limit_bytes=LIMIT * MIB),
        cost_estimate=pl.CostEstimate(flops=1_000_000, bytes_accessed=MIB // 4, transcendentals=0),
    )(spot, *rows, *pieces, *(before or ()))


def finish_kernel(spot, own, across, side, *refs):
    out = refs[-1]
    mine = spot[1] & 1
    for i, part in enumerate((own, across)):
        for kind in range(2):
            for head in range(KVH):
                value = part[kind, head] + side[i, kind, head].astype(jnp.float32)
                if kind == 0:
                    value = value * refs[2 * i][...] + pltpu.roll(value, HD // 2, 1) * refs[2 * i + 1][...]
                out[mine ^ i, head, kind] = value.astype(jnp.bfloat16)


def finish(spot, own, across, side, angles):
    out = pl.pallas_call(
        finish_kernel,
        out_shape=jax.ShapeDtypeStruct((2, KVH, 2, 256, HD), jnp.bfloat16),
        in_specs=[SMEM] + [VMEM] * (3 + len(angles)),
        out_specs=VMEM,
        compiler_params=pltpu.CompilerParams(vmem_limit_bytes=8 * MIB),
        cost_estimate=pl.CostEstimate(flops=4_000_000, bytes_accessed=MIB, transcendentals=0),
    )(spot, own, across, side, *angles)
    return out.reshape(16, 2, 256, HD)


def cache_of(received, kind):
    blocks = [
        (received[i, kind].astype(jnp.float32) + received[8 + i, kind].astype(jnp.float32)).reshape(B, 8, HD)
        for i in range(8)
    ]
    return jnp.stack(blocks, axis=1).reshape(B, 64, HD)


def split(value):
    high = value.astype(jnp.bfloat16)
    return high, (value - high.astype(jnp.float32)).astype(jnp.bfloat16)


NT = (((1,), (1,)), ((), ()))


def line_of(peak, total):
    row = lax.broadcasted_iota(jnp.int32, (2 * ROWS, 128), 0)
    lane = lax.broadcasted_iota(jnp.int32, (2 * ROWS, 128), 1)
    line = jnp.where(row == lane, peak, 0.0) + jnp.where(row + 64 == lane, total, 0.0)
    line = jnp.sum(line, axis=0, keepdims=True)
    high = line.astype(jnp.bfloat16).astype(jnp.float32)
    middle = (line - high).astype(jnp.bfloat16).astype(jnp.float32)
    at = lax.broadcasted_iota(jnp.int32, (16, 128), 0)
    terms = jnp.where(at == 0, high, jnp.where(at == 1, middle, line - high - middle))
    return jnp.where(at < 3, terms, 0.0).astype(jnp.bfloat16)


def scored(query, keys, length, column):
    both = lax.dot_general(jnp.concatenate(split(query), 0), keys, NT, preferred_element_type=jnp.float32)
    return jnp.where(column < length, (both[:ROWS] + both[ROWS:]) * (1.0 / math.sqrt(HD)), -1e30)


def weighted(weight, values):
    both = jnp.dot(jnp.concatenate(split(weight), 0), values, preferred_element_type=jnp.float32)
    return both[:ROWS] + both[ROWS:]


def attend_kernel(spot, lengths, received, query, fresh_keys, fresh_values, keys, values, packed, scores):
    seq = spot[4]
    keys[...] = cache_of(received, 0).astype(jnp.bfloat16)
    values[...] = cache_of(received, 1).astype(jnp.bfloat16)
    column = lax.broadcasted_iota(jnp.int32, (ROWS, 64), 1) + seq * 64
    for b in range(B):
        scores[pl.ds(ROWS * b, ROWS)] = scored(query[b], keys[b], lengths[b], column)
    score = scores[...]
    peak = jnp.max(score, axis=1, keepdims=True)
    weight = jnp.where(score > -1e29, jnp.exp(score - peak), 0.0)
    total = jnp.sum(weight, axis=1, keepdims=True)
    for b in range(B):
        mixed = weighted(weight[ROWS * b : ROWS * b + ROWS], values[b])
        packed[b // 2, pl.ds(ROWS * (b % 2), ROWS)] = mixed.astype(jnp.bfloat16)
    for pair in range(B // 2):
        rows = slice(2 * ROWS * pair, 2 * ROWS * pair + 2 * ROWS)
        packed[pair, pl.ds(64, 16)] = line_of(peak[rows], total[rows])

    late = lax.broadcasted_iota(jnp.int32, (ROWS, 8), 1)
    token = lax.broadcasted_iota(jnp.int32, (ROWS, 8), 0) // GROUP
    peaks, totals = [], []
    for i in range(2):
        b = 2 * seq + i
        score = scored(query[b], keys[b], lengths[b], column)
        late_score = (1.0 / math.sqrt(HD)) * lax.dot_general(
            query[b], fresh_keys[b], NT, preferred_element_type=jnp.float32, precision=lax.Precision.HIGHEST
        )
        late_score = jnp.where(late <= token, late_score, -1e30)
        peak = jnp.maximum(jnp.max(score, axis=1, keepdims=True), jnp.max(late_score, axis=1, keepdims=True))
        weight = jnp.where(score > -1e29, jnp.exp(score - peak), 0.0)
        late_weight = jnp.where(late <= token, jnp.exp(late_score - peak), 0.0)
        mixed = weighted(weight, values[b]) + weighted(late_weight, fresh_values[b])
        packed[seq, pl.ds(ROWS * i, ROWS)] = mixed.astype(jnp.bfloat16)
        peaks.append(peak)
        totals.append(jnp.sum(weight, axis=1, keepdims=True) + jnp.sum(late_weight, axis=1, keepdims=True))
    packed[seq, pl.ds(64, 16)] = line_of(jnp.concatenate(peaks, 0), jnp.concatenate(totals, 0))


def attend(spot, lengths, received, query, fresh_keys, fresh_values):
    return pl.pallas_call(
        attend_kernel,
        out_shape=(
            jax.ShapeDtypeStruct((B, 64, HD), jnp.bfloat16),
            jax.ShapeDtypeStruct((B, 64, HD), jnp.bfloat16),
            jax.ShapeDtypeStruct((B // 2, 80, HD), jnp.bfloat16),
        ),
        in_specs=[SMEM, SMEM] + [VMEM] * 4,
        out_specs=[VMEM] * 3,
        scratch_shapes=[pltpu.VMEM((B * ROWS, 64), jnp.float32)],
        compiler_params=pltpu.CompilerParams(vmem_limit_bytes=16 * MIB),
        cost_estimate=pl.CostEstimate(flops=60_000_000, bytes_accessed=4 * MIB, transcendentals=70_000),
    )(spot, lengths, received, query, fresh_keys, fresh_values)


def merge_kernel(parts, out):
    lines = [jnp.sum(parts[i, 64:80].astype(jnp.float32), axis=0, keepdims=True) for i in range(16)]
    marks = jnp.concatenate(lines, 0)
    lane = lax.broadcasted_iota(jnp.int32, (16, 128), 1)
    peak = jnp.max(marks, axis=0, keepdims=True)
    grow = jnp.where(lane < 64, jnp.exp(marks - peak), 0.0)
    total = jnp.sum(grow * pltpu.roll(marks, 64, 1), axis=0, keepdims=True)
    share = grow / jnp.where(lane[:1] < 64, total, 1.0)
    columns = jnp.concatenate([share, jnp.zeros((112, 128), jnp.float32)], 0).T
    result = sum(parts[i, :64].astype(jnp.float32) * columns[:64, i : i + 1] for i in range(16))
    for i in range(STEPS):
        rows = [
            jnp.concatenate(
                [result[at + r : at + r + 1] for r in range(GROUP)], 1
            )
            for at in (GROUP * i, ROWS + GROUP * i)
        ]
        out[i] = jnp.concatenate(rows, 0).astype(jnp.bfloat16)


def merge(parts):
    return pl.pallas_call(
        merge_kernel,
        out_shape=jax.ShapeDtypeStruct((STEPS, 2, GROUP * HD), jnp.bfloat16),
        in_specs=[VMEM],
        out_specs=VMEM,
        cost_estimate=pl.CostEstimate(flops=300_000, bytes_accessed=MIB, transcendentals=2048),
    )(parts)


def shards(context_hidden, norm_gain, kv_weight, queries, new_kv, lengths, slab_start):
    seq, head = lax.axis_index(SEQ), lax.axis_index(HEAD)
    z, ylo, core = seq >> 2, (seq >> 1) & 1, seq & 1
    x, yhi = head >> 1, head & 1
    spot = jnp.stack([x, yhi * 2 + ylo, z, core, seq]).astype(jnp.int32)

    weight = jnp.stack([kv_weight, lax.ppermute(kv_weight, AXES, flipped(y=2))])
    own_rows, to_side, to_across, to_corner = prep(
        spot, context_hidden.reshape(256, 8192), norm_gain.reshape(1, 8192)
    )
    weight, own_rows = together(weight, own_rows)
    corner_rows = lax.ppermute(to_corner, AXES, flipped(y=1))
    across_rows = lax.ppermute(to_across, AXES, flipped(y=1))
    side_rows = lax.ppermute(to_side, AXES, flipped(core=1))
    middle, last = (Z, X), (X, Z)
    halves = [weight[:, :, :HALF], weight[:, :, HALF:]]
    firsts = [swap(half, dim, 0) for half, dim in zip(halves, middle)]
    firsts = together(*firsts)
    pairs = [jnp.stack(pair) for pair in zip(halves, firsts)]
    seconds = [swap(pair, dim, 1) for pair, dim in zip(pairs, middle)]
    blocks = [jnp.concatenate(both) for both in zip(pairs, seconds)]
    _, side_rows, queries, new_kv, slab_start = together(blocks[0], side_rows, queries, new_kv, slab_start)

    one = [swap(block, dim, 0) for block, dim in zip(blocks, last)]
    two = [swap(block, dim, 1) for block, dim in zip(blocks, last)]
    freqs = rope_freqs()
    angles = ()
    for near in (seq, seq ^ 2):
        position = slab_start[:, None] + (near * 8 + head) * 8 + jnp.arange(8, dtype=jnp.int32)[None, :]
        angles += tables(position.reshape(256), freqs)
    step_pos = (slab_start + lengths)[:, None] + jnp.arange(STEPS, dtype=jnp.int32)[None, :]
    step_cos, step_sin = tables(step_pos, freqs)
    query = queries.astype(jnp.float32).reshape(STEPS, B, GROUP, HD).transpose(1, 0, 2, 3)
    query = rotated(query, step_cos[:, :, None], step_sin[:, :, None]).reshape(B, ROWS, HD)
    fresh = new_kv.astype(jnp.float32).transpose(0, 2, 1, 3)
    padding = ((0, 0), (0, 8 - STEPS), (0, 0))
    fresh_keys = jnp.pad(rotated(fresh[0], step_cos, step_sin), padding)
    fresh_values = jnp.pad(new_kv[1].transpose(1, 0, 2), padding)
    own, side = product(spot, [own_rows, side_rows], blocks, (0,))
    far = [swap(block, dim, 1) for block, dim in zip(one, last)]
    one, two, corner_rows, own, side, query, fresh_keys, fresh_values, angles = together(
        one, two, corner_rows, own, side, query, fresh_keys, fresh_values, angles
    )
    corner_rows = lax.ppermute(corner_rows, AXES, flipped(core=1))

    own, side = product(spot, [own_rows, side_rows], [*one, *two], (1, 2), [own, side])
    spot_later, own, side = together(spot, own, side)
    corner, across = product(spot_later, [corner_rows, across_rows], [*blocks, *one, *two], (0, 1, 2))
    (sent,) = product(spot, [side_rows, corner_rows], far, (3,), [side, corner], narrow=True)
    side = lax.ppermute(sent, AXES, flipped(core=1))
    own, across = product(spot, [own_rows, across_rows], far, (3,), [own, across])
    rows = finish(spot, own, across, side, angles)
    received = lax.all_to_all(rows, ("ylo", "x", "yhi"), 0, 0)
    k_cache, v_cache, packed = attend(spot, lengths, received, query, fresh_keys, fresh_values)
    parts = lax.all_to_all(packed, SEQ, 0, 0)
    attention = merge(parts)
    return k_cache, v_cache, attention


def solution(mesh):
    fine = Mesh(mesh.devices.reshape(4, 2, 2, 4, 2), AXES)
    return jax.shard_map(
        shards,
        mesh=fine,
        in_specs=(
            P(None, AXES, None),
            P(),
            P(None, SEQ, HEAD),
            P(None, None, HEAD),
            P(None, None, None, HEAD),
            P(),
            P(),
        ),
        out_specs=(P(None, SEQ, HEAD), P(None, SEQ, HEAD), P(None, SEQ, HEAD)),
        check_vma=False,
    )
```

```python
import functools
import math

import jax
import jax.numpy as jnp
from jax import lax
from jax.experimental import pallas as pl
from jax.experimental.pallas import tpu as pltpu
from jax.sharding import Mesh
from jax.sharding import PartitionSpec as P

HQ = 64
KVH = 8
HD = 128
STEPS = 4
B = 32
GROUP = HQ // KVH
ROWS = STEPS * GROUP
AXES = ("z", "ylo", "core", "x", "yhi")
SEQ, HEAD = AXES[:3], AXES[3:]
X, Y, Z = 0, 1, 2
MIB = 1024 * 1024
LIMIT = 12
VMEM = pl.BlockSpec(memory_space=pltpu.VMEM)
SMEM = pl.BlockSpec(memory_space=pltpu.SMEM)

HALF = 256


def place(n):
    s, h = n >> 3, n & 7
    return [h >> 1, (h & 1) * 2 + ((s >> 1) & 1), s >> 2, s & 1]


def flat(x, y, z, core):
    return (((z * 2 + (y & 1)) * 2 + core) * 4 + x) * 2 + (y >> 1)


def exchange(dim, step):
    pairs = []
    for n in range(128):
        spot = place(n)
        spot[dim] ^= (1, 3)[spot[3] ^ step]
        pairs.append((flat(*spot), n))
    return pairs


def flipped(x=0, y=0, core=0):
    pairs = []
    for n in range(128):
        spot = place(n)
        pairs.append((flat(spot[0] ^ x, spot[1] ^ y, spot[2], spot[3] ^ core), n))
    return pairs


def swap(value, dim, step):
    return lax.ppermute(value, AXES, exchange(dim, step))


def together(*values):
    return lax.optimization_barrier(values)


def doubled(block, dim):
    pair = jnp.stack([block, swap(block, dim, 0)])
    return jnp.concatenate([pair, swap(pair, dim, 1)])


def rope_freqs():
    indices = jnp.arange(HD // 2, dtype=jnp.float32)
    base_freq = jnp.exp(-2.0 * indices / HD * math.log(500000.0))
    wavelength = 2.0 * math.pi / base_freq
    blend_weight = (8192.0 / wavelength - 1.0) / 3.0
    middle = (1.0 - blend_weight) * base_freq / 8.0 + blend_weight * base_freq
    return jnp.where(
        wavelength > 8192.0, base_freq / 8.0, jnp.where(wavelength < 2048.0, base_freq, middle)
    )


def tables(position, freqs):
    angles = position.astype(jnp.float32)[..., None] * freqs
    cosine, sine = jnp.cos(angles), jnp.sin(angles)
    return jnp.concatenate([cosine, cosine], -1), jnp.concatenate([-sine, sine], -1)


def rotated(vectors, cosine, sine):
    half = HD // 2
    swapped = jnp.concatenate([vectors[..., half:], vectors[..., :half]], -1)
    return vectors * cosine + swapped * sine


def prep_kernel(spot, hidden, gain, own, side, across, corner, rows, total, sems):
    mine = 2 * (spot[1] & 1) + spot[3]
    copies = []
    for i in range(4):
        lanes = pl.ds(2048 * i, 2048)
        copies.append(pltpu.make_async_copy(hidden.at[:, lanes], rows.at[:, lanes], sems.at[i]))
        copies[i].start()
    for i in range(4):
        copies[i].wait()

        def add(tile, _, i=i):
            at = pl.ds(pl.multiple_of(16 * tile, 16), 16)
            part = 0.0 if i == 0 else total[at, :]
            for lane in range(2048 * i, 2048 * i + 2048, 128):
                x = rows[at, lane : lane + 128].astype(jnp.float32)
                part = part + x * x
            total[at, :] = part
            return 0

        lax.fori_loop(0, 16, add, 0)
    mean = jnp.sum(total[...], axis=1, keepdims=True) / 8192.0
    total[...] = jnp.broadcast_to(lax.rsqrt(mean + 1e-05), (256, 128))
    for owner in range(4):

        @pl.when(mine == owner)
        def _():
            outs = (own, side, across, corner)

            def write(tile, _):
                at = pl.ds(pl.multiple_of(16 * tile, 16), 16)
                scale = total[at, :]
                for lane in range(0, 8192, 128):
                    z, quarter, half, rest = lane // 2048, lane // 512 % 4, lane // HALF % 2, lane % HALF
                    x = rows[at, lane : lane + 128].astype(jnp.float32)
                    x = x * scale * gain[:, lane : lane + 128]
                    to = 1024 * half + HALF * z + rest
                    outs[quarter ^ owner][at, to : to + 128] = x.astype(jnp.bfloat16)
                return 0

            lax.fori_loop(0, 16, write, 0)


def prep(spot, hidden, gain):
    return pl.pallas_call(
        prep_kernel,
        out_shape=[jax.ShapeDtypeStruct((256, 2048), jnp.bfloat16)] * 4,
        in_specs=[SMEM, pl.BlockSpec(memory_space=pl.ANY), VMEM],
        out_specs=[VMEM] * 4,
        scratch_shapes=[
            pltpu.VMEM((256, 8192), jnp.bfloat16),
            pltpu.VMEM((256, 128), jnp.float32),
            pltpu.SemaphoreType.DMA((4,)),
        ],
        compiler_params=pltpu.CompilerParams(vmem_limit_bytes=48 * MIB),
        cost_estimate=pl.CostEstimate(flops=1_000_000, bytes_accessed=MIB // 4, transcendentals=0),
    )(spot, hidden, gain)


def product_kernel(slots, inputs, carried, narrow, spot, *refs):
    x_refs, refs = refs[:inputs], refs[inputs:]
    piece_refs, refs = refs[: 2 * len(slots)], refs[2 * len(slots) :]
    if carried:
        before, refs = refs[:inputs], refs[inputs:]
    if narrow:
        out = refs[0]
    else:
        sums = refs
    mine = [spot[0], spot[1], spot[2]]
    core = spot[3]
    flips = [0, 1 + 2 * core, 3 - 2 * core, 2]

    def slot_of(flip):
        return jnp.where(flip == 0, 0, jnp.where(flip == flips[1], 1, jnp.where(flip == flips[2], 2, 3)))

    z_slots = [slot_of(z ^ mine[Z]) for z in range(4)]
    yhi = [mine[Y] >> 1, 1 - (mine[Y] >> 1)]
    places = [(ys, kind) for ys in range(2) for kind in range(2)]
    for xs in range(4):
        lanes, weight = [], []
        for i, slot in enumerate(slots):
            ref = piece_refs[2 * i + 1]
            z = mine[Z] ^ flips[slot]
            lanes.append(pl.ds(pl.multiple_of(1024 + HALF * z, HALF), HALF))
            weight.append(jnp.concatenate([ref[xs, ys, kind] for ys, kind in places], 1))
            if slot == xs:
                ref = piece_refs[2 * i]
                lanes.append(pl.ds(0, 1024))
                weight += [jnp.concatenate([ref[s, ys, kind] for ys, kind in places], 1) for s in z_slots]
        weight = jnp.concatenate(weight, 0)
        x = mine[X] ^ flips[xs]
        left = jnp.concatenate([jnp.concatenate([rows[:, at] for rows in x_refs], 0) for at in lanes], 1)
        result = jnp.dot(left, weight, preferred_element_type=jnp.float32)
        for n in range(inputs):
            for i, (ys, kind) in enumerate(places):
                value = result[256 * n : 256 * n + 256, 128 * i : 128 * i + 128]
                if carried:
                    value = value + before[n][kind, 2 * x + yhi[ys]]
                if narrow:
                    out[n, kind, 2 * x + yhi[ys]] = value.astype(out.dtype)
                else:
                    sums[n][kind, 2 * x + yhi[ys]] = value


def product(spot, rows, pieces, slots, before=None, narrow=False):
    carried = before is not None
    shape = (2, KVH, 256, HD)
    count = len(rows)
    if narrow:
        out_shape = [jax.ShapeDtypeStruct((count, *shape), jnp.bfloat16)]
    else:
        out_shape = [jax.ShapeDtypeStruct(shape, jnp.float32)] * count
    return pl.pallas_call(
        functools.partial(product_kernel, slots, count, carried, narrow),
        out_shape=out_shape,
        in_specs=[SMEM] + [VMEM] * (count + len(pieces) + (count if carried else 0)),
        out_specs=[VMEM] * len(out_shape),
        compiler_params=pltpu.CompilerParams(vmem_limit_bytes=LIMIT * MIB),
        cost_estimate=pl.CostEstimate(flops=1_000_000, bytes_accessed=MIB // 4, transcendentals=0),
    )(spot, *rows, *pieces, *(before or ()))


def finish_kernel(spot, own, across, side, *refs):
    out = refs[-1]
    mine = spot[1] & 1
    for i, part in enumerate((own, across)):
        for kind in range(2):
            for head in range(KVH):
                value = part[kind, head] + side[i, kind, head].astype(jnp.float32)
                if kind == 0:
                    value = value * refs[2 * i][...] + pltpu.roll(value, HD // 2, 1) * refs[2 * i + 1][...]
                out[mine ^ i, head, kind] = value.astype(jnp.bfloat16)


def finish(spot, own, across, side, angles):
    out = pl.pallas_call(
        finish_kernel,
        out_shape=jax.ShapeDtypeStruct((2, KVH, 2, 256, HD), jnp.bfloat16),
        in_specs=[SMEM] + [VMEM] * (3 + len(angles)),
        out_specs=VMEM,
        compiler_params=pltpu.CompilerParams(vmem_limit_bytes=8 * MIB),
        cost_estimate=pl.CostEstimate(flops=4_000_000, bytes_accessed=MIB, transcendentals=0),
    )(spot, own, across, side, *angles)
    return out.reshape(16, 2, 256, HD)


def cache_of(received, kind):
    blocks = [
        (received[i, kind].astype(jnp.float32) + received[8 + i, kind].astype(jnp.float32)).reshape(B, 8, HD)
        for i in range(8)
    ]
    return jnp.stack(blocks, axis=1).reshape(B, 64, HD)


def split(value):
    high = value.astype(jnp.bfloat16)
    return high, (value - high.astype(jnp.float32)).astype(jnp.bfloat16)


NT = (((1,), (1,)), ((), ()))


def line_of(peak, total):
    row = lax.broadcasted_iota(jnp.int32, (2 * ROWS, 128), 0)
    lane = lax.broadcasted_iota(jnp.int32, (2 * ROWS, 128), 1)
    line = jnp.where(row == lane, peak, 0.0) + jnp.where(row + 64 == lane, total, 0.0)
    line = jnp.sum(line, axis=0, keepdims=True)
    high = line.astype(jnp.bfloat16).astype(jnp.float32)
    middle = (line - high).astype(jnp.bfloat16).astype(jnp.float32)
    at = lax.broadcasted_iota(jnp.int32, (16, 128), 0)
    terms = jnp.where(at == 0, high, jnp.where(at == 1, middle, line - high - middle))
    return jnp.where(at < 3, terms, 0.0).astype(jnp.bfloat16)


def scored(query, keys, length, column):
    both = lax.dot_general(jnp.concatenate(split(query), 0), keys, NT, preferred_element_type=jnp.float32)
    return jnp.where(column < length, (both[:ROWS] + both[ROWS:]) * (1.0 / math.sqrt(HD)), -1e30)


def weighted(weight, values):
    both = jnp.dot(jnp.concatenate(split(weight), 0), values, preferred_element_type=jnp.float32)
    return both[:ROWS] + both[ROWS:]


def attend_kernel(spot, lengths, received, query, fresh_keys, fresh_values, keys, values, packed, scores):
    seq = spot[4]
    keys[...] = cache_of(received, 0).astype(jnp.bfloat16)
    values[...] = cache_of(received, 1).astype(jnp.bfloat16)
    column = lax.broadcasted_iota(jnp.int32, (ROWS, 64), 1) + seq * 64
    for b in range(B):
        scores[pl.ds(ROWS * b, ROWS)] = scored(query[b], keys[b], lengths[b], column)
    score = scores[...]
    peak = jnp.max(score, axis=1, keepdims=True)
    weight = jnp.where(score > -1e29, jnp.exp(score - peak), 0.0)
    total = jnp.sum(weight, axis=1, keepdims=True)
    for b in range(B):
        mixed = weighted(weight[ROWS * b : ROWS * b + ROWS], values[b])
        packed[b // 2, pl.ds(ROWS * (b % 2), ROWS)] = mixed.astype(jnp.bfloat16)
    for pair in range(B // 2):
        rows = slice(2 * ROWS * pair, 2 * ROWS * pair + 2 * ROWS)
        packed[pair, pl.ds(64, 16)] = line_of(peak[rows], total[rows])

    late = lax.broadcasted_iota(jnp.int32, (ROWS, 8), 1)
    token = lax.broadcasted_iota(jnp.int32, (ROWS, 8), 0) // GROUP
    peaks, totals = [], []
    for i in range(2):
        b = 2 * seq + i
        score = scored(query[b], keys[b], lengths[b], column)
        late_score = (1.0 / math.sqrt(HD)) * lax.dot_general(
            query[b], fresh_keys[b], NT, preferred_element_type=jnp.float32, precision=lax.Precision.HIGHEST
        )
        late_score = jnp.where(late <= token, late_score, -1e30)
        peak = jnp.maximum(jnp.max(score, axis=1, keepdims=True), jnp.max(late_score, axis=1, keepdims=True))
        weight = jnp.where(score > -1e29, jnp.exp(score - peak), 0.0)
        late_weight = jnp.where(late <= token, jnp.exp(late_score - peak), 0.0)
        mixed = weighted(weight, values[b]) + weighted(late_weight, fresh_values[b])
        packed[seq, pl.ds(ROWS * i, ROWS)] = mixed.astype(jnp.bfloat16)
        peaks.append(peak)
        totals.append(jnp.sum(weight, axis=1, keepdims=True) + jnp.sum(late_weight, axis=1, keepdims=True))
    packed[seq, pl.ds(64, 16)] = line_of(jnp.concatenate(peaks, 0), jnp.concatenate(totals, 0))


def attend(spot, lengths, received, query, fresh_keys, fresh_values):
    return pl.pallas_call(
        attend_kernel,
        out_shape=(
            jax.ShapeDtypeStruct((B, 64, HD), jnp.bfloat16),
            jax.ShapeDtypeStruct((B, 64, HD), jnp.bfloat16),
            jax.ShapeDtypeStruct((B // 2, 80, HD), jnp.bfloat16),
        ),
        in_specs=[SMEM, SMEM] + [VMEM] * 4,
        out_specs=[VMEM] * 3,
        scratch_shapes=[pltpu.VMEM((B * ROWS, 64), jnp.float32)],
        compiler_params=pltpu.CompilerParams(vmem_limit_bytes=16 * MIB),
        cost_estimate=pl.CostEstimate(flops=60_000_000, bytes_accessed=4 * MIB, transcendentals=70_000),
    )(spot, lengths, received, query, fresh_keys, fresh_values)


def merge_kernel(parts, out):
    lines = [jnp.sum(parts[i, 64:80].astype(jnp.float32), axis=0, keepdims=True) for i in range(16)]
    marks = jnp.concatenate(lines, 0)
    lane = lax.broadcasted_iota(jnp.int32, (16, 128), 1)
    peak = jnp.max(marks, axis=0, keepdims=True)
    grow = jnp.where(lane < 64, jnp.exp(marks - peak), 0.0)
    total = jnp.sum(grow * pltpu.roll(marks, 64, 1), axis=0, keepdims=True)
    share = grow / jnp.where(lane[:1] < 64, total, 1.0)
    columns = jnp.concatenate([share, jnp.zeros((112, 128), jnp.float32)], 0).T
    result = sum(parts[i, :64].astype(jnp.float32) * columns[:64, i : i + 1] for i in range(16))
    for i in range(STEPS):
        rows = [
            jnp.concatenate(
                [result[at + r : at + r + 1] for r in range(GROUP)], 1
            )
            for at in (GROUP * i, ROWS + GROUP * i)
        ]
        out[i] = jnp.concatenate(rows, 0).astype(jnp.bfloat16)


def merge(parts):
    return pl.pallas_call(
        merge_kernel,
        out_shape=jax.ShapeDtypeStruct((STEPS, 2, GROUP * HD), jnp.bfloat16),
        in_specs=[VMEM],
        out_specs=VMEM,
        cost_estimate=pl.CostEstimate(flops=300_000, bytes_accessed=MIB, transcendentals=2048),
    )(parts)


def shards(context_hidden, norm_gain, kv_weight, queries, new_kv, lengths, slab_start):
    seq, head = lax.axis_index(SEQ), lax.axis_index(HEAD)
    z, ylo, core = seq >> 2, (seq >> 1) & 1, seq & 1
    x, yhi = head >> 1, head & 1
    spot = jnp.stack([x, yhi * 2 + ylo, z, core, seq]).astype(jnp.int32)

    weight = jnp.stack([kv_weight, lax.ppermute(kv_weight, AXES, flipped(y=2))])
    own_rows, to_side, to_across, to_corner = prep(
        spot, context_hidden.reshape(256, 8192), norm_gain.reshape(1, 8192)
    )
    weight, own_rows = together(weight, own_rows)
    corner_rows = lax.ppermute(to_corner, AXES, flipped(y=1))
    across_rows = lax.ppermute(to_across, AXES, flipped(y=1))
    side_rows = lax.ppermute(to_side, AXES, flipped(core=1))
    middle, last = (Z, X), (X, Z)
    halves = [weight[:, :, :HALF], weight[:, :, HALF:]]
    firsts = [swap(half, dim, 0) for half, dim in zip(halves, middle)]
    firsts = together(*firsts)
    pairs = [jnp.stack(pair) for pair in zip(halves, firsts)]
    seconds = [swap(pair, dim, 1) for pair, dim in zip(pairs, middle)]
    blocks = [jnp.concatenate(both) for both in zip(pairs, seconds)]
    _, side_rows, queries, new_kv, slab_start = together(blocks[0], side_rows, queries, new_kv, slab_start)

    one = [swap(block, dim, 0) for block, dim in zip(blocks, last)]
    two = [swap(block, dim, 1) for block, dim in zip(blocks, last)]
    freqs = rope_freqs()
    angles = ()
    for near in (seq, seq ^ 2):
        position = slab_start[:, None] + (near * 8 + head) * 8 + jnp.arange(8, dtype=jnp.int32)[None, :]
        angles += tables(position.reshape(256), freqs)
    step_pos = (slab_start + lengths)[:, None] + jnp.arange(STEPS, dtype=jnp.int32)[None, :]
    step_cos, step_sin = tables(step_pos, freqs)
    query = queries.astype(jnp.float32).reshape(STEPS, B, GROUP, HD).transpose(1, 0, 2, 3)
    query = rotated(query, step_cos[:, :, None], step_sin[:, :, None]).reshape(B, ROWS, HD)
    fresh = new_kv.astype(jnp.float32).transpose(0, 2, 1, 3)
    padding = ((0, 0), (0, 8 - STEPS), (0, 0))
    fresh_keys = jnp.pad(rotated(fresh[0], step_cos, step_sin), padding)
    fresh_values = jnp.pad(new_kv[1].transpose(1, 0, 2), padding)
    own, side = product(spot, [own_rows, side_rows], blocks, (0,))
    far = [swap(block, dim, 1) for block, dim in zip(one, last)]
    one, corner_rows, own, side, query, fresh_keys, fresh_values, angles = together(
        one, corner_rows, own, side, query, fresh_keys, fresh_values, angles
    )
    corner_rows = lax.ppermute(corner_rows, AXES, flipped(core=1))

    own, side = product(spot, [own_rows, side_rows], one, (1,), [own, side])
    spot_two, own, side = together(spot, own, side)
    own, side = product(spot_two, [own_rows, side_rows], two, (2,), [own, side])
    spot_later, own, side = together(spot, own, side)
    corner, across = product(spot_later, [corner_rows, across_rows], [*blocks, *one, *two], (0, 1, 2))
    (sent,) = product(spot, [side_rows, corner_rows], far, (3,), [side, corner], narrow=True)
    side = lax.ppermute(sent, AXES, flipped(core=1))
    own, across = product(spot, [own_rows, across_rows], far, (3,), [own, across])
    rows = finish(spot, own, across, side, angles)
    received = lax.all_to_all(rows, ("ylo", "x", "yhi"), 0, 0)
    k_cache, v_cache, packed = attend(spot, lengths, received, query, fresh_keys, fresh_values)
    parts = lax.all_to_all(packed, SEQ, 0, 0)
    attention = merge(parts)
    return k_cache, v_cache, attention


def solution(mesh):
    fine = Mesh(mesh.devices.reshape(4, 2, 2, 4, 2), AXES)
    return jax.shard_map(
        shards,
        mesh=fine,
        in_specs=(
            P(None, AXES, None),
            P(),
            P(None, SEQ, HEAD),
            P(None, None, HEAD),
            P(None, None, None, HEAD),
            P(),
            P(),
        ),
        out_specs=(P(None, SEQ, HEAD), P(None, SEQ, HEAD), P(None, SEQ, HEAD)),
        check_vma=False,
    )
```

```python
import functools
import math

import jax
import jax.numpy as jnp
from jax import lax
from jax.experimental import pallas as pl
from jax.experimental.pallas import tpu as pltpu
from jax.sharding import Mesh
from jax.sharding import PartitionSpec as P

HQ = 64
KVH = 8
HD = 128
STEPS = 4
B = 32
GROUP = HQ // KVH
ROWS = STEPS * GROUP
AXES = ("z", "ylo", "core", "x", "yhi")
SEQ, HEAD = AXES[:3], AXES[3:]
X, Y, Z = 0, 1, 2
MIB = 1024 * 1024
LIMIT = 12
VMEM = pl.BlockSpec(memory_space=pltpu.VMEM)
SMEM = pl.BlockSpec(memory_space=pltpu.SMEM)

HALF = 256


def place(n):
    s, h = n >> 3, n & 7
    return [h >> 1, (h & 1) * 2 + ((s >> 1) & 1), s >> 2, s & 1]


def flat(x, y, z, core):
    return (((z * 2 + (y & 1)) * 2 + core) * 4 + x) * 2 + (y >> 1)


def exchange(dim, step):
    pairs = []
    for n in range(128):
        spot = place(n)
        spot[dim] ^= (1, 3)[spot[3] ^ step]
        pairs.append((flat(*spot), n))
    return pairs


def flipped(x=0, y=0, core=0):
    pairs = []
    for n in range(128):
        spot = place(n)
        pairs.append((flat(spot[0] ^ x, spot[1] ^ y, spot[2], spot[3] ^ core), n))
    return pairs


def swap(value, dim, step):
    return lax.ppermute(value, AXES, exchange(dim, step))


def together(*values):
    return lax.optimization_barrier(values)


def doubled(block, dim):
    pair = jnp.stack([block, swap(block, dim, 0)])
    return jnp.concatenate([pair, swap(pair, dim, 1)])


def rope_freqs():
    indices = jnp.arange(HD // 2, dtype=jnp.float32)
    base_freq = jnp.exp(-2.0 * indices / HD * math.log(500000.0))
    wavelength = 2.0 * math.pi / base_freq
    blend_weight = (8192.0 / wavelength - 1.0) / 3.0
    middle = (1.0 - blend_weight) * base_freq / 8.0 + blend_weight * base_freq
    return jnp.where(
        wavelength > 8192.0, base_freq / 8.0, jnp.where(wavelength < 2048.0, base_freq, middle)
    )


def tables(position, freqs):
    angles = position.astype(jnp.float32)[..., None] * freqs
    cosine, sine = jnp.cos(angles), jnp.sin(angles)
    return jnp.concatenate([cosine, cosine], -1), jnp.concatenate([-sine, sine], -1)


def rotated(vectors, cosine, sine):
    half = HD // 2
    swapped = jnp.concatenate([vectors[..., half:], vectors[..., :half]], -1)
    return vectors * cosine + swapped * sine


def prep_kernel(spot, hidden, gain, own, side, across, corner, rows, total, sems):
    mine = 2 * (spot[1] & 1) + spot[3]
    copies = []
    for i in range(4):
        lanes = pl.ds(2048 * i, 2048)
        copies.append(pltpu.make_async_copy(hidden.at[:, lanes], rows.at[:, lanes], sems.at[i]))
        copies[i].start()
    for i in range(4):
        copies[i].wait()

        def add(tile, _, i=i):
            at = pl.ds(pl.multiple_of(16 * tile, 16), 16)
            part = 0.0 if i == 0 else total[at, :]
            for lane in range(2048 * i, 2048 * i + 2048, 128):
                x = rows[at, lane : lane + 128].astype(jnp.float32)
                part = part + x * x
            total[at, :] = part
            return 0

        lax.fori_loop(0, 16, add, 0)
    mean = jnp.sum(total[...], axis=1, keepdims=True) / 8192.0
    total[...] = jnp.broadcast_to(lax.rsqrt(mean + 1e-05), (256, 128))
    for owner in range(4):

        @pl.when(mine == owner)
        def _():
            outs = (own, side, across, corner)

            def write(tile, _):
                at = pl.ds(pl.multiple_of(16 * tile, 16), 16)
                scale = total[at, :]
                for lane in range(0, 8192, 128):
                    z, quarter, half, rest = lane // 2048, lane // 512 % 4, lane // HALF % 2, lane % HALF
                    x = rows[at, lane : lane + 128].astype(jnp.float32)
                    x = x * scale * gain[:, lane : lane + 128]
                    to = 1024 * half + HALF * z + rest
                    outs[quarter ^ owner][at, to : to + 128] = x.astype(jnp.bfloat16)
                return 0

            lax.fori_loop(0, 16, write, 0)


def prep(spot, hidden, gain):
    return pl.pallas_call(
        prep_kernel,
        out_shape=[jax.ShapeDtypeStruct((256, 2048), jnp.bfloat16)] * 4,
        in_specs=[SMEM, pl.BlockSpec(memory_space=pl.ANY), VMEM],
        out_specs=[VMEM] * 4,
        scratch_shapes=[
            pltpu.VMEM((256, 8192), jnp.bfloat16),
            pltpu.VMEM((256, 128), jnp.float32),
            pltpu.SemaphoreType.DMA((4,)),
        ],
        compiler_params=pltpu.CompilerParams(vmem_limit_bytes=48 * MIB),
        cost_estimate=pl.CostEstimate(flops=1_000_000, bytes_accessed=MIB // 4, transcendentals=0),
    )(spot, hidden, gain)


def product_kernel(slots, inputs, carried, narrow, spot, *refs):
    x_refs, refs = refs[:inputs], refs[inputs:]
    piece_refs, refs = refs[: 2 * len(slots)], refs[2 * len(slots) :]
    if carried:
        before, refs = refs[:inputs], refs[inputs:]
    if narrow:
        out = refs[0]
    else:
        sums = refs
    mine = [spot[0], spot[1], spot[2]]
    core = spot[3]
    flips = [0, 1 + 2 * core, 3 - 2 * core, 2]

    def slot_of(flip):
        return jnp.where(flip == 0, 0, jnp.where(flip == flips[1], 1, jnp.where(flip == flips[2], 2, 3)))

    z_slots = [slot_of(z ^ mine[Z]) for z in range(4)]
    yhi = [mine[Y] >> 1, 1 - (mine[Y] >> 1)]
    places = [(ys, kind) for ys in range(2) for kind in range(2)]
    for xs in range(4):
        lanes, weight = [], []
        for i, slot in enumerate(slots):
            ref = piece_refs[2 * i + 1]
            z = mine[Z] ^ flips[slot]
            lanes.append(pl.ds(pl.multiple_of(1024 + HALF * z, HALF), HALF))
            weight.append(jnp.concatenate([ref[xs, ys, kind] for ys, kind in places], 1))
            if slot == xs:
                ref = piece_refs[2 * i]
                lanes.append(pl.ds(0, 1024))
                weight += [jnp.concatenate([ref[s, ys, kind] for ys, kind in places], 1) for s in z_slots]
        weight = jnp.concatenate(weight, 0)
        x = mine[X] ^ flips[xs]
        left = jnp.concatenate([jnp.concatenate([rows[:, at] for rows in x_refs], 0) for at in lanes], 1)
        result = jnp.dot(left, weight, preferred_element_type=jnp.float32)
        for n in range(inputs):
            for i, (ys, kind) in enumerate(places):
                value = result[256 * n : 256 * n + 256, 128 * i : 128 * i + 128]
                if carried:
                    value = value + before[n][kind, 2 * x + yhi[ys]]
                if narrow:
                    out[n, kind, 2 * x + yhi[ys]] = value.astype(out.dtype)
                else:
                    sums[n][kind, 2 * x + yhi[ys]] = value


def product(spot, rows, pieces, slots, before=None, narrow=False):
    carried = before is not None
    shape = (2, KVH, 256, HD)
    count = len(rows)
    if narrow:
        out_shape = [jax.ShapeDtypeStruct((count, *shape), jnp.bfloat16)]
    else:
        out_shape = [jax.ShapeDtypeStruct(shape, jnp.float32)] * count
    return pl.pallas_call(
        functools.partial(product_kernel, slots, count, carried, narrow),
        out_shape=out_shape,
        in_specs=[SMEM] + [VMEM] * (count + len(pieces) + (count if carried else 0)),
        out_specs=[VMEM] * len(out_shape),
        compiler_params=pltpu.CompilerParams(vmem_limit_bytes=LIMIT * MIB),
        cost_estimate=pl.CostEstimate(flops=1_000_000, bytes_accessed=MIB // 4, transcendentals=0),
    )(spot, *rows, *pieces, *(before or ()))


def finish_kernel(spot, own, across, side, *refs):
    out = refs[-1]
    mine = spot[1] & 1
    for i, part in enumerate((own, across)):
        for kind in range(2):
            for head in range(KVH):
                value = part[kind, head] + side[i, kind, head].astype(jnp.float32)
                if kind == 0:
                    value = value * refs[2 * i][...] + pltpu.roll(value, HD // 2, 1) * refs[2 * i + 1][...]
                out[mine ^ i, head, kind] = value.astype(jnp.bfloat16)


def finish(spot, own, across, side, angles):
    out = pl.pallas_call(
        finish_kernel,
        out_shape=jax.ShapeDtypeStruct((2, KVH, 2, 256, HD), jnp.bfloat16),
        in_specs=[SMEM] + [VMEM] * (3 + len(angles)),
        out_specs=VMEM,
        compiler_params=pltpu.CompilerParams(vmem_limit_bytes=8 * MIB),
        cost_estimate=pl.CostEstimate(flops=4_000_000, bytes_accessed=MIB, transcendentals=0),
    )(spot, own, across, side, *angles)
    return out.reshape(16, 2, 256, HD)


def cache_of(received, kind):
    blocks = [
        (received[i, kind].astype(jnp.float32) + received[8 + i, kind].astype(jnp.float32)).reshape(B, 8, HD)
        for i in range(8)
    ]
    return jnp.stack(blocks, axis=1).reshape(B, 64, HD)


def split(value):
    high = value.astype(jnp.bfloat16)
    return high, (value - high.astype(jnp.float32)).astype(jnp.bfloat16)


NT = (((1,), (1,)), ((), ()))


def line_of(peak, total):
    row = lax.broadcasted_iota(jnp.int32, (2 * ROWS, 128), 0)
    lane = lax.broadcasted_iota(jnp.int32, (2 * ROWS, 128), 1)
    line = jnp.where(row == lane, peak, 0.0) + jnp.where(row + 64 == lane, total, 0.0)
    line = jnp.sum(line, axis=0, keepdims=True)
    high = line.astype(jnp.bfloat16).astype(jnp.float32)
    middle = (line - high).astype(jnp.bfloat16).astype(jnp.float32)
    at = lax.broadcasted_iota(jnp.int32, (16, 128), 0)
    terms = jnp.where(at == 0, high, jnp.where(at == 1, middle, line - high - middle))
    return jnp.where(at < 3, terms, 0.0).astype(jnp.bfloat16)


def scored(query, keys, length, column):
    both = lax.dot_general(jnp.concatenate(split(query), 0), keys, NT, preferred_element_type=jnp.float32)
    return jnp.where(column < length, (both[:ROWS] + both[ROWS:]) * (1.0 / math.sqrt(HD)), -1e30)


def weighted(weight, values):
    both = jnp.dot(jnp.concatenate(split(weight), 0), values, preferred_element_type=jnp.float32)
    return both[:ROWS] + both[ROWS:]


def attend_kernel(spot, lengths, received, query, fresh_keys, fresh_values, keys, values, packed, scores):
    seq = spot[4]
    keys[...] = cache_of(received, 0).astype(jnp.bfloat16)
    values[...] = cache_of(received, 1).astype(jnp.bfloat16)
    column = lax.broadcasted_iota(jnp.int32, (ROWS, 64), 1) + seq * 64
    for b in range(B):
        scores[pl.ds(ROWS * b, ROWS)] = scored(query[b], keys[b], lengths[b], column)
    score = scores[...]
    peak = jnp.max(score, axis=1, keepdims=True)
    weight = jnp.where(score > -1e29, jnp.exp(score - peak), 0.0)
    total = jnp.sum(weight, axis=1, keepdims=True)
    for b in range(B):
        mixed = weighted(weight[ROWS * b : ROWS * b + ROWS], values[b])
        packed[b // 2, pl.ds(ROWS * (b % 2), ROWS)] = mixed.astype(jnp.bfloat16)
    for pair in range(B // 2):
        rows = slice(2 * ROWS * pair, 2 * ROWS * pair + 2 * ROWS)
        packed[pair, pl.ds(64, 16)] = line_of(peak[rows], total[rows])

    late = lax.broadcasted_iota(jnp.int32, (ROWS, 8), 1)
    token = lax.broadcasted_iota(jnp.int32, (ROWS, 8), 0) // GROUP
    peaks, totals = [], []
    for i in range(2):
        b = 2 * seq + i
        score = scored(query[b], keys[b], lengths[b], column)
        late_score = (1.0 / math.sqrt(HD)) * lax.dot_general(
            query[b], fresh_keys[b], NT, preferred_element_type=jnp.float32, precision=lax.Precision.HIGHEST
        )
        late_score = jnp.where(late <= token, late_score, -1e30)
        peak = jnp.maximum(jnp.max(score, axis=1, keepdims=True), jnp.max(late_score, axis=1, keepdims=True))
        weight = jnp.where(score > -1e29, jnp.exp(score - peak), 0.0)
        late_weight = jnp.where(late <= token, jnp.exp(late_score - peak), 0.0)
        mixed = weighted(weight, values[b]) + weighted(late_weight, fresh_values[b])
        packed[seq, pl.ds(ROWS * i, ROWS)] = mixed.astype(jnp.bfloat16)
        peaks.append(peak)
        totals.append(jnp.sum(weight, axis=1, keepdims=True) + jnp.sum(late_weight, axis=1, keepdims=True))
    packed[seq, pl.ds(64, 16)] = line_of(jnp.concatenate(peaks, 0), jnp.concatenate(totals, 0))


def attend(spot, lengths, received, query, fresh_keys, fresh_values):
    return pl.pallas_call(
        attend_kernel,
        out_shape=(
            jax.ShapeDtypeStruct((B, 64, HD), jnp.bfloat16),
            jax.ShapeDtypeStruct((B, 64, HD), jnp.bfloat16),
            jax.ShapeDtypeStruct((B // 2, 80, HD), jnp.bfloat16),
        ),
        in_specs=[SMEM, SMEM] + [VMEM] * 4,
        out_specs=[VMEM] * 3,
        scratch_shapes=[pltpu.VMEM((B * ROWS, 64), jnp.float32)],
        compiler_params=pltpu.CompilerParams(vmem_limit_bytes=16 * MIB),
        cost_estimate=pl.CostEstimate(flops=60_000_000, bytes_accessed=4 * MIB, transcendentals=70_000),
    )(spot, lengths, received, query, fresh_keys, fresh_values)


def merge_kernel(parts, out):
    lines = [jnp.sum(parts[i, 64:80].astype(jnp.float32), axis=0, keepdims=True) for i in range(16)]
    marks = jnp.concatenate(lines, 0)
    lane = lax.broadcasted_iota(jnp.int32, (16, 128), 1)
    peak = jnp.max(marks, axis=0, keepdims=True)
    grow = jnp.where(lane < 64, jnp.exp(marks - peak), 0.0)
    total = jnp.sum(grow * pltpu.roll(marks, 64, 1), axis=0, keepdims=True)
    share = grow / jnp.where(lane[:1] < 64, total, 1.0)
    columns = jnp.concatenate([share, jnp.zeros((112, 128), jnp.float32)], 0).T
    result = sum(parts[i, :64].astype(jnp.float32) * columns[:64, i : i + 1] for i in range(16))
    for i in range(STEPS):
        rows = [
            jnp.concatenate(
                [result[at + r : at + r + 1] for r in range(GROUP)], 1
            )
            for at in (GROUP * i, ROWS + GROUP * i)
        ]
        out[i] = jnp.concatenate(rows, 0).astype(jnp.bfloat16)


def merge(parts):
    return pl.pallas_call(
        merge_kernel,
        out_shape=jax.ShapeDtypeStruct((STEPS, 2, GROUP * HD), jnp.bfloat16),
        in_specs=[VMEM],
        out_specs=VMEM,
        cost_estimate=pl.CostEstimate(flops=300_000, bytes_accessed=MIB, transcendentals=2048),
    )(parts)


def shards(context_hidden, norm_gain, kv_weight, queries, new_kv, lengths, slab_start):
    seq, head = lax.axis_index(SEQ), lax.axis_index(HEAD)
    z, ylo, core = seq >> 2, (seq >> 1) & 1, seq & 1
    x, yhi = head >> 1, head & 1
    spot = jnp.stack([x, yhi * 2 + ylo, z, core, seq]).astype(jnp.int32)

    weight = jnp.stack([kv_weight, lax.ppermute(kv_weight, AXES, flipped(y=2))])
    own_rows, to_side, to_across, to_corner = prep(
        spot, context_hidden.reshape(256, 8192), norm_gain.reshape(1, 8192)
    )
    weight, own_rows = together(weight, own_rows)
    corner_rows = lax.ppermute(to_corner, AXES, flipped(y=1))
    corner_rows, to_across = together(corner_rows, to_across)
    across_rows = lax.ppermute(to_across, AXES, flipped(y=1))
    side_rows = lax.ppermute(to_side, AXES, flipped(core=1))
    middle, last = (Z, X), (X, Z)
    halves = [weight[:, :, :HALF], weight[:, :, HALF:]]
    firsts = [swap(half, dim, 0) for half, dim in zip(halves, middle)]
    firsts = together(*firsts)
    pairs = [jnp.stack(pair) for pair in zip(halves, firsts)]
    seconds = [swap(pair, dim, 1) for pair, dim in zip(pairs, middle)]
    blocks = [jnp.concatenate(both) for both in zip(pairs, seconds)]
    _, side_rows, queries, new_kv, slab_start = together(blocks[0], side_rows, queries, new_kv, slab_start)

    one = [swap(block, dim, 0) for block, dim in zip(blocks, last)]
    two = [swap(block, dim, 1) for block, dim in zip(blocks, last)]
    freqs = rope_freqs()
    angles = ()
    for near in (seq, seq ^ 2):
        position = slab_start[:, None] + (near * 8 + head) * 8 + jnp.arange(8, dtype=jnp.int32)[None, :]
        angles += tables(position.reshape(256), freqs)
    step_pos = (slab_start + lengths)[:, None] + jnp.arange(STEPS, dtype=jnp.int32)[None, :]
    step_cos, step_sin = tables(step_pos, freqs)
    query = queries.astype(jnp.float32).reshape(STEPS, B, GROUP, HD).transpose(1, 0, 2, 3)
    query = rotated(query, step_cos[:, :, None], step_sin[:, :, None]).reshape(B, ROWS, HD)
    fresh = new_kv.astype(jnp.float32).transpose(0, 2, 1, 3)
    padding = ((0, 0), (0, 8 - STEPS), (0, 0))
    fresh_keys = jnp.pad(rotated(fresh[0], step_cos, step_sin), padding)
    fresh_values = jnp.pad(new_kv[1].transpose(1, 0, 2), padding)
    corner_rows = lax.ppermute(corner_rows, AXES, flipped(core=1))
    own, side = product(spot, [own_rows, side_rows], blocks, (0,))
    far = [swap(block, dim, 1) for block, dim in zip(one, last)]
    one, corner_rows, own, side, query, fresh_keys, fresh_values, angles = together(
        one, corner_rows, own, side, query, fresh_keys, fresh_values, angles
    )

    own, side = product(spot, [own_rows, side_rows], one, (1,), [own, side])
    spot_two, own, side = together(spot, own, side)
    own, side = product(spot_two, [own_rows, side_rows], two, (2,), [own, side])
    spot_later, own, side = together(spot, own, side)
    corner, across = product(spot_later, [corner_rows, across_rows], [*blocks, *one, *two], (0, 1, 2))
    (sent,) = product(spot, [side_rows, corner_rows], far, (3,), [side, corner], narrow=True)
    side = lax.ppermute(sent, AXES, flipped(core=1))
    own, across = product(spot, [own_rows, across_rows], far, (3,), [own, across])
    rows = finish(spot, own, across, side, angles)
    received = lax.all_to_all(rows, ("ylo", "x", "yhi"), 0, 0)
    k_cache, v_cache, packed = attend(spot, lengths, received, query, fresh_keys, fresh_values)
    parts = lax.all_to_all(packed, SEQ, 0, 0)
    attention = merge(parts)
    return k_cache, v_cache, attention


def solution(mesh):
    fine = Mesh(mesh.devices.reshape(4, 2, 2, 4, 2), AXES)
    return jax.shard_map(
        shards,
        mesh=fine,
        in_specs=(
            P(None, AXES, None),
            P(),
            P(None, SEQ, HEAD),
            P(None, None, HEAD),
            P(None, None, None, HEAD),
            P(),
            P(),
        ),
        out_specs=(P(None, SEQ, HEAD), P(None, SEQ, HEAD), P(None, SEQ, HEAD)),
        check_vma=False,
    )
```
